512 devices in a mesh: gx: 8 (over z_lo, core), vert: 64 (over y, x, z_hi).
Axes of the slice: x: 4, y: 4, z: 16 (z_hi: 4, z_lo: 4; z = z_hi * 4 + z_lo), core: 2. Of those that a mesh axis runs over, the one named last changes fastest.
Arguments:
- density_start: float32 [64, 16, 16, 32, 128], P('vert', None, None, 'gx'), may hold values from 0.05 to 18, as said below
- value_guess: float32 [64, 16, 16, 32, 128], P('vert', None, None, 'gx'), may hold values from -6 to 6
- value_end: float32 [64, 16, 16, 32, 128], P('vert', None, None, 'gx'), may hold values from -6 to 6
- walls: int32 [32, 128], P('gx'), may hold values from 0 to 1, as said below
Outputs:
- density_end: float32 [64, 16, 16, 32, 128], P('vert', None, None, 'gx')
- value_start: float32 [64, 16, 16, 32, 128], P('vert', None, None, 'gx')
The draws below stay inside these ranges and needn't reach their ends.
Inputs may be any that keep to these rules, and one draw needn't show every extreme that they name: `walls`: each row of fixed x holds exactly 32 wall cells. `density_start`: A positive density.
All inputs are finite; a program needn't handle non-finite values.
Results may differ from the reference program's by a relative error of at most 0.00002.
Values sent between devices are 32-bit elements; how exact they have to be, the bound alone decides.
A program may use at most 64 MiB of HBM per device.

```python
import math
import jax
import jax.numpy as jnp
from jax import lax

VX = 128
VY = 128
KY = 8
KX = 8
BX = 16
BY = 16
NY = 128
NX = 32
WALL = 32


def draw_density_start(key, part):
    key = jax.random.fold_in(key, 11)
    cell_key, space_key = jax.random.split(key)
    fraction = (jnp.arange(VX, dtype=jnp.float32) / (VX - 1)).reshape(VX, 1, 1, 1)
    cells = jnp.exp(jax.random.uniform(cell_key, (VX, VY, NX, NY), jnp.float32, math.log(0.5), math.log(2.0)))
    space = jnp.exp(jax.random.uniform(space_key, (NX, NY), jnp.float32, math.log(0.3), math.log(3.0)))
    rising = 1.0 + 2.0 * fraction
    full = cells * space * rising
    return full.reshape(KX, BX, KY, BY, NX, NY).transpose(0, 2, 1, 3, 4, 5).reshape(KX * KY, BX, BY, NX, NY)


def draw_walls(key, part):
    key = jax.random.fold_in(key, 23)
    scores = jax.random.randint(key, (NX, NY), 0, 2 ** 20) * NY + jnp.arange(NY, dtype=jnp.int32)[None, :]
    ranks = jnp.argsort(jnp.argsort(scores, axis=1), axis=1)
    return (ranks < WALL).astype(jnp.int32)


def levels(key, extent, pieces, low, top_value):
    gain = 1.0
    for position, parts in pieces:
        heights = jax.random.uniform(jax.random.fold_in(jax.random.fold_in(key, 6), position), (parts,), jnp.float32, low / len(pieces), top_value / len(pieces))
        gain = gain * jnp.repeat(jnp.exp(heights), extent[position] // parts).reshape((-1,) + (1,) * (len(extent) - 1 - position))
    return gain


def centred(rng, extent, deviation, reach, pieces=(), held_as=jnp.bfloat16):
    gain = levels(rng, extent, pieces, -0.22, 0.18) if pieces else 1.0
    values = jax.random.normal(rng, extent, jnp.float32) * deviation * gain
    return jnp.minimum(jnp.maximum(values, -reach), reach).astype(held_as)


def setup_inputs(seed: int = 0) -> dict:
    key_of = jax.random.split(jax.random.key(seed), 5)
    return {
        "density_start": draw_density_start(jax.random.fold_in(key_of[4], 71), 0),
        "value_guess": centred(key_of[1], (KX * KY, BX, BY, NX, NY), 1.0, 6.0, ((0, 64), (3, 8)), jnp.float32),
        "value_end": centred(key_of[2], (KX * KY, BX, BY, NX, NY), 1.0, 6.0, ((0, 64), (3, 8)), jnp.float32),
        "walls": draw_walls(jax.random.fold_in(key_of[4], 71), 0),
    }


advect_rate = 0.3
diffusion = 0.05
drift_limit = 0.1
control_gain = 1.0
alignment = 1.0
hamilton_rate = 0.05
time_step = 0.2
density_cost = 2.0
velocity_cost = 1.0


def to_full(blocked):
    return blocked.reshape(KX, KY, BX, BY, NX, NY).transpose(0, 2, 1, 3, 4, 5).reshape(VX, VY, NX, NY)


def to_blocks(field):
    return field.reshape(KX, BX, KY, BY, NX, NY).transpose(0, 2, 1, 3, 4, 5).reshape(KX * KY, BX, BY, NX, NY)


def lower(field, along):
    widths = [(0, 0)] * 4
    widths[along] = (1, 0)
    return lax.slice_in_dim(jnp.pad(field, widths), 0, field.shape[along], axis=along)


def upper(field, along):
    widths = [(0, 0)] * 4
    widths[along] = (0, 1)
    return lax.slice_in_dim(jnp.pad(field, widths), 1, field.shape[along] + 1, axis=along)


def moments(field, vx_hat, vy_hat):
    total = jnp.sum(field, axis=(0, 1))
    mom_x = jnp.sum(vx_hat * field, axis=(0, 1))
    mom_y = jnp.sum(vy_hat * field, axis=(0, 1))
    return total, mom_x / total, mom_y / total


def reflect(field, wall_cells):
    return jnp.where(wall_cells, 0.5 * (field + field[:, ::-1]), field)


def forward_step(field, grad_x, grad_y, stats, vx_hat, vy_hat, wall_cells):
    total, mean_x, mean_y = stats
    drift_x = drift_limit * jnp.tanh(-control_gain * grad_x + alignment * (mean_x - vx_hat))
    drift_y = drift_limit * jnp.tanh(-control_gain * grad_y + alignment * (mean_y - vy_hat))
    push_x = jnp.maximum(drift_x, 0.0) * field
    pull_x = jnp.minimum(drift_x, 0.0) * field
    push_y = jnp.maximum(drift_y, 0.0) * field
    pull_y = jnp.minimum(drift_y, 0.0) * field
    spread = diffusion * field
    velocity_part = (lower(spread + push_x, 0) + upper(spread - pull_x, 0) + lower(spread + push_y, 1)
                     + upper(spread - pull_y, 1) - 4.0 * spread - push_x + pull_x - push_y + pull_y)
    speed_x = advect_rate * vx_hat
    speed_y = advect_rate * vy_hat
    transport = (jnp.maximum(speed_x, 0.0) * (field - jnp.roll(field, 1, axis=2))
                 + jnp.minimum(speed_x, 0.0) * (jnp.roll(field, -1, axis=2) - field)
                 + jnp.maximum(speed_y, 0.0) * (field - jnp.roll(field, 1, axis=3))
                 + jnp.minimum(speed_y, 0.0) * (jnp.roll(field, -1, axis=3) - field))
    return reflect(field + velocity_part - transport, wall_cells)


def backward_step(value, stats, vx_hat, vy_hat, wall_cells):
    total, mean_x, mean_y = stats
    below_x = lower(value, 0)
    above_x = upper(value, 0)
    below_y = lower(value, 1)
    above_y = upper(value, 1)
    grad_x = 0.5 * (above_x - below_x)
    grad_y = 0.5 * (above_y - below_y)
    laplace = above_x + below_x + above_y + below_y - 4.0 * value
    speed_x = advect_rate * vx_hat
    speed_y = advect_rate * vy_hat
    transport = (jnp.maximum(speed_x, 0.0) * (jnp.roll(value, -1, axis=2) - value)
                 + jnp.minimum(speed_x, 0.0) * (value - jnp.roll(value, 1, axis=2))
                 + jnp.maximum(speed_y, 0.0) * (jnp.roll(value, -1, axis=3) - value)
                 + jnp.minimum(speed_y, 0.0) * (value - jnp.roll(value, 1, axis=3)))
    density = total / (VX * VY)
    offset_x = vx_hat - mean_x
    offset_y = vy_hat - mean_y
    running = density_cost * density + 0.5 * velocity_cost * (offset_x * offset_x + offset_y * offset_y)
    updated = (value + transport - hamilton_rate * (grad_x * grad_x + grad_y * grad_y)
               + diffusion * laplace + time_step * running)
    return reflect(updated, wall_cells)


def reference(density_start, value_guess, value_end, walls):
    vx_hat = ((jnp.arange(VX, dtype=jnp.float32) - (VX - 1) / 2.0) / (VX / 2.0)).reshape(VX, 1, 1, 1)
    vy_hat = ((jnp.arange(VY, dtype=jnp.float32) - (VY - 1) / 2.0) / (VY / 2.0)).reshape(1, VY, 1, 1)
    wall_cells = (walls == 1)[None, None]
    guess = to_full(value_guess)
    grad_x = 0.5 * (upper(guess, 0) - lower(guess, 0))
    grad_y = 0.5 * (upper(guess, 1) - lower(guess, 1))
    field = to_full(density_start)
    stats_start = moments(field, vx_hat, vy_hat)
    field_one = forward_step(field, grad_x, grad_y, stats_start, vx_hat, vy_hat, wall_cells)
    stats_one = moments(field_one, vx_hat, vy_hat)
    field_two = forward_step(field_one, grad_x, grad_y, stats_one, vx_hat, vy_hat, wall_cells)
    stats_two = moments(field_two, vx_hat, vy_hat)
    value_one = backward_step(to_full(value_end), stats_two, vx_hat, vy_hat, wall_cells)
    value_zero = backward_step(value_one, stats_one, vx_hat, vy_hat, wall_cells)
    return to_blocks(field_two), to_blocks(value_zero)
```

```python
import functools

import jax
import jax.numpy as jnp
from jax import lax
from jax.experimental import pallas as pl
from jax.experimental.pallas import tpu as pltpu
from jax.sharding import PartitionSpec as P

MESH = pl.DeviceIdType.MESH
F32 = jnp.float32

VX = 128
VY = 128
KX = 8
KY = 8
BX = 16
BY = 16
TILES = 8
PACK = 4

advect_rate = 0.3
diffusion = 0.05
drift_limit = 0.1
hamilton_rate = 0.05
time_step = 0.2
density_cost = 2.0
velocity_cost = 1.0


def roll4(a):
    return pltpu.roll(a, 4, axis=a.ndim - 2)


def kernel(
    m_ref, g_ref, u_ref, walls_ref, mo_ref, vo_ref,
    mext, mext2, gext, gradx, grady, gradh, upx, dnx, field, uext, vext, pre, wz,
    hy, xh, ylo, yhi, ysend, xsend, gvy, csend, crecv, red, tiles, idx,
    send_sem, recv_sem,
):
    vert = lax.axis_index("vert")
    gx = lax.axis_index("gx")
    gx_count = lax.axis_size("gx")
    i = vert // KY
    j = vert % KY
    zh = vert % 4
    px = (vert // 4) % 4
    py = vert // 16

    def at(y, x, z):
        return {"vert": ((y % 4) * 4 + x % 4) * 4 + z % 4}

    plane = [at(py + d // 4, px + d % 4, zh) for d in range(1, 16)]
    depth = [at(py, px, zh + d) for d in range(1, 4)]
    mirror = {"vert": i * KY + (KY - 1 - j)}
    vx_up = {"vert": ((i + 1) % KX) * KY + j}
    vx_down = {"vert": ((i + KX - 1) % KX) * KY + j}
    vy_up = {"vert": i * KY + (j + 1) % KY}
    vy_down = {"vert": i * KY + (j + KY - 1) % KY}
    x_up = {"gx": (gx + 1) % gx_count}
    x_down = {"gx": (gx + gx_count - 1) % gx_count}

    barrier = pltpu.get_barrier_semaphore()
    roles = plane + depth + [mirror, vy_up, vy_down, x_up, x_down]
    for peer in roles:
        pl.semaphore_signal(barrier, inc=1, device_id=peer, device_id_type=MESH)

    row = lax.broadcasted_iota(jnp.int32, (8, 128), 0)
    lane = lax.broadcasted_iota(jnp.int32, (8, 128), 1)
    lo8 = row < 4
    high_x = i >= KX // 2
    high_y = j >= KY // 2

    def vx_hat(e):
        return ((i * BX + e).astype(F32) - (VX - 1) / 2.0) / (VX / 2.0)

    shape = (TILES, 8, 128)
    vy_row = 2 * lax.broadcasted_iota(jnp.int32, shape, 0) + lax.broadcasted_iota(jnp.int32, shape, 1) // 4
    vy_hat = ((j * BY + vy_row).astype(F32) - (VY - 1) / 2.0) / (VY / 2.0)
    vy_edge = jnp.where(lo8, j * BY - 1, j * BY + BY)
    vy_hat_edge = (vy_edge.astype(F32) - (VY - 1) / 2.0) / (VY / 2.0)
    inside_edge = (vy_edge >= 0) & (vy_edge < VY)
    speed_y = jnp.abs(advect_rate * vy_hat)

    def local_moments(read):
        def body(vx, carry):
            total, mom_x, mom_y = carry
            slab = read(vx)
            s = jnp.sum(slab, axis=0)
            return (total + s, mom_x + vx_hat(vx) * s, mom_y + jnp.sum(vy_hat * slab, axis=0))

        zero = jnp.zeros((8, 128), F32)
        return lax.fori_loop(0, BX, body, (zero, zero, zero))

    def put_moments(slot, sums):
        total, mom_x, mom_y = (a + roll4(a) for a in sums)
        red[slot, 0] = jnp.where(lo8, total, mom_x)
        red[slot, 1] = mom_y

    put_moments(0, local_moments(lambda vx: m_ref[vx]))

    w4 = walls_ref[...]
    wall = jnp.concatenate([w4, w4], axis=0) == 1
    ones = wall.astype(F32)
    sub128 = lax.broadcasted_iota(jnp.int32, (128, 128), 0)
    lane128 = lax.broadcasted_iota(jnp.int32, (128, 128), 1)
    upto = (sub128 <= lane128).astype(F32)
    count = jnp.dot(ones, upto, preferred_element_type=F32)
    count_t = lax.dot_general(
        (lane128 <= sub128).astype(F32), ones, (((1,), (1,)), ((), ())), preferred_element_type=F32
    )
    rank = jnp.clip(count.astype(jnp.int32) - 1, 0, 31)
    nth = (lane128 % 32).astype(F32)
    pick = jnp.zeros((8, 128), F32)
    for x in range(4):
        place = jnp.sum((count_t[:, x : x + 1] <= nth).astype(F32), axis=0, keepdims=True)
        pick = jnp.where(row % 4 == x, place, pick)
    idx[0] = jnp.minimum(pick.astype(jnp.int32), 127)
    idx[1] = rank

    def along_y(slab, index):
        return jnp.take_along_axis(slab, jnp.broadcast_to(index[None], shape), axis=2)

    pl.semaphore_wait(barrier, len(roles))

    counter = [0]

    def copy(src, dst, peer):
        n = counter[0]
        counter[0] += 1
        return pltpu.make_async_remote_copy(
            src_ref=src, dst_ref=dst, send_sem=send_sem.at[n], recv_sem=recv_sem.at[n],
            device_id=peer, device_id_type=MESH,
        )

    sent = []

    def start(src, dst, peer):
        c = copy(src, dst, peer)
        c.start()
        sent.append(c)
        return c

    def arrive(copies):
        for c in copies:
            c.wait_recv()

    def plane_start(r):
        base = 20 * r
        return [start(red.at[base], red.at[base + 1 + d], peer) for d, peer in enumerate(plane)]

    def plane_finish(r, copies):
        base = 20 * r
        arrive(copies)
        acc = red[base]
        for d in range(15):
            acc = acc + red[base + 1 + d]
        red[base + 16] = acc
        return [start(red.at[base + 16], red.at[base + 17 + d], peer) for d, peer in enumerate(depth)]

    def depth_finish(r, copies, reflected):
        base = 20 * r
        arrive(copies)
        acc = red[base + 16]
        for d in range(3):
            acc = acc + red[base + 17 + d]
        swapped = roll4(acc[0])
        total = jnp.where(lo8, acc[0], swapped)
        mom_x = jnp.where(lo8, swapped, acc[0])
        mean_y = acc[1] / total
        if reflected:
            mean_y = jnp.where(wall, 0.0, mean_y)
        return total, mom_x / total, mean_y

    def vy_faces(slot, read):
        def body(p, _):
            a0, a1 = read(2 * p, TILES - 1), read(2 * p + 1, TILES - 1)
            ysend[slot, p] = jnp.where(lo8, roll4(a0), a1)
            b0, b1 = read(2 * p, 0), read(2 * p + 1, 0)
            ysend[slot + 1, p] = jnp.where(lo8, b0, roll4(b1))
            return 0

        lax.fori_loop(0, BX // 2, body, 0)
        return [
            start(ysend.at[slot], ylo.at[slot // 2], vy_up),
            start(ysend.at[slot + 1], yhi.at[slot // 2], vy_down),
        ]

    def vy_halo(slot, copies):
        arrive(copies)

        def body(p, _):
            low, high = ylo[slot // 2, p], yhi[slot // 2, p]
            hy[slot // 2, 2 * p] = jnp.where(inside_edge, jnp.where(lo8, low, roll4(high)), 0.0)
            hy[slot // 2, 2 * p + 1] = jnp.where(inside_edge, jnp.where(lo8, roll4(low), high), 0.0)
            return 0

        lax.fori_loop(0, BX // 2, body, 0)

    def vx_faces(ext):
        return [
            start(ext.at[BX], ext.at[0], vx_up),
            start(ext.at[1], ext.at[BX + 1], vx_down),
        ]

    def vx_halo(ext, copies):
        arrive(copies)
        ext[0] = jnp.where(i == 0, 0.0, ext[0])
        ext[BX + 1] = jnp.where(i == KX - 1, 0.0, ext[BX + 1])

    def x_faces(slot, read, below):
        def body(q, _):
            face = None
            for b in range(PACK):
                slab = read(PACK * q + b)
                moved = jnp.where(below, pltpu.roll(slab, (b - 3) % 8, axis=1), pltpu.roll(slab, (b + 3) % 8, axis=1))
                target = jnp.where(below, b, b + 3) % 4
                face = moved if face is None else jnp.where((row % 4 == target)[None], moved, face)
            xsend[slot, q] = face
            return 0

        lax.fori_loop(0, BX // PACK, body, 0)

    def x_neighbour(slab, slot, q, b, below):
        shifted = jnp.where(below, pltpu.roll(slab, 1, axis=1), pltpu.roll(slab, 7, axis=1))
        edge = row % 4 == jnp.where(below, 0, 3)
        return jnp.where(edge[None], pltpu.roll(xh[slot, q], (8 - b) % 8, axis=1), shifted)

    def y_neighbour(slab, below):
        return pltpu.roll(slab, jnp.where(below, 1, 127), axis=2)

    def vy_neighbours(low, high, edge_low, edge_high):
        r_low, r_high = roll4(low), roll4(high)
        lower = jnp.where(lo8[None], jnp.concatenate([edge_low[None], r_low[:-1]], axis=0), r_low)
        upper = jnp.where(lo8[None], r_high, jnp.concatenate([r_high[1:], edge_high[None]], axis=0))
        return lower, upper

    def both_vy(slab, edge):
        r = roll4(slab)
        lower = jnp.where(lo8[None], jnp.concatenate([edge[None], r[:-1]], axis=0), r)
        upper = jnp.where(lo8[None], r, jnp.concatenate([r[1:], edge[None]], axis=0))
        return lower, upper

    def mirror_copies(slot):
        n = counter[0]
        counter[0] += PACK

        def make(q):
            return pltpu.make_async_remote_copy(
                src_ref=csend.at[slot, q], dst_ref=crecv.at[slot, q],
                send_sem=send_sem.at[n + q], recv_sem=recv_sem.at[n + q],
                device_id=mirror, device_id_type=MESH,
            )

        return make

    def packed(face, slab, b):
        taken = along_y(slab, idx[0])
        return taken if face is None else jnp.where((lane // 32 == b)[None], taken, face)

    def send_packed(slot, q, face, make):
        turned = roll4(face)
        for t in range(TILES):
            csend[slot, q, t] = turned[TILES - 1 - t]
        make(q).start()

    def reflect(slot, make, read, write):
        def body(q, carry):
            make(q).wait_recv()
            face = crecv[slot, q]
            for b in range(PACK):
                vx = PACK * q + b
                slab = read(vx)
                other = along_y(face, idx[1] + 32 * b)
                write(vx, jnp.where(wall[None], 0.5 * (slab + other), slab))
            return carry

        lax.fori_loop(0, PACK, body, 0)

    def forward(ext, slot, xslot, stats, write, cslot):
        total, mean_x, mean_y = stats

        def rates(e, _):
            cells = ext[e]
            drift = drift_limit * jnp.tanh((mean_x - vx_hat(e - 1))[None] - gradx[e])
            upx[e] = cells * (diffusion + jnp.maximum(drift, 0.0))
            dnx[e] = cells * (diffusion + jnp.maximum(-drift, 0.0))
            return 0

        lax.fori_loop(0, BX + 2, rates, 0)
        make = mirror_copies(cslot)

        def body(q, carry):
            total, mom_x, mom_y = carry
            face = None
            for b in range(PACK):
                vx = PACK * q + b
                cells = ext[vx + 1]
                drift = drift_limit * jnp.tanh(mean_y[None] - vy_hat - grady[vx])
                up = cells * (diffusion + jnp.maximum(drift, 0.0))
                down = cells * (diffusion + jnp.maximum(-drift, 0.0))
                drift_e = drift_limit * jnp.tanh(mean_y - vy_hat_edge - gradh[vx])
                cells_e = hy[slot // 2, vx]
                up_e = cells_e * (diffusion + jnp.maximum(drift_e, 0.0))
                down_e = cells_e * (diffusion + jnp.maximum(-drift_e, 0.0))
                lower, upper = vy_neighbours(up, down, up_e, down_e)
                flow = upx[vx] + dnx[vx + 2] + lower + upper - (upx[vx + 1] + dnx[vx + 1] + up + down)
                speed_x = jnp.abs(advect_rate * vx_hat(vx))
                moved = speed_x * (cells - x_neighbour(cells, xslot, q, b, high_x))
                moved = moved + speed_y * (cells - y_neighbour(cells, high_y))
                new = cells + flow - moved
                write(vx, new)
                s = jnp.sum(new, axis=0)
                total = total + s
                mom_x = mom_x + vx_hat(vx) * s
                mom_y = mom_y + jnp.sum(vy_hat * new, axis=0)
                face = packed(face, new, b)
            send_packed(cslot, q, face, make)
            return total, mom_x, mom_y

        zero = jnp.zeros((8, 128), F32)
        sums = lax.fori_loop(0, PACK, body, (zero, zero, zero))
        return sums, make

    plane0 = plane_start(0)

    def fill(ext, ref, lead):
        def body(vx, _):
            ext[vx + lead] = ref[vx]
            return 0

        lax.fori_loop(0, BX, body, 0)

    fill(uext, u_ref, 1)
    u_vx = vx_faces(uext)
    u_vy = vy_faces(0, lambda vx, t: u_ref[vx, t])
    x_faces(0, lambda vx: u_ref[vx], jnp.logical_not(high_x))

    def x_send(slot, below):
        peer = {"gx": jnp.where(below, (gx + 1) % gx_count, (gx + gx_count - 1) % gx_count)}
        return start(xsend.at[slot], xh.at[slot], peer)

    u_x = x_send(0, jnp.logical_not(high_x))
    fill(gext, g_ref, 2)
    g_vx = [
        start(gext.at[pl.ds(BX, 2)], gext.at[pl.ds(0, 2)], vx_up),
        start(gext.at[pl.ds(2, 2)], gext.at[pl.ds(BX + 2, 2)], vx_down),
    ]
    fill(mext, m_ref, 1)
    m_vx = vx_faces(mext)
    m_vy = vy_faces(2, lambda vx, t: m_ref[vx, t])
    x_faces(1, lambda vx: m_ref[vx], high_x)
    m_x = x_send(1, high_x)

    def fill_g(vx, _):
        gvy[0, vx] = g_ref[vx, TILES - 1]
        gvy[1, vx] = g_ref[vx, 0]
        return 0

    lax.fori_loop(0, BX, fill_g, 0)
    g_vy = [start(gvy.at[0], gvy.at[2], vy_up), start(gvy.at[1], gvy.at[3], vy_down)]

    depth0 = plane_finish(0, plane0)

    vx_halo(uext, u_vx)
    vy_halo(0, u_vy)
    arrive([u_x])
    make_u = mirror_copies(0)

    def value_step(q, _):
        face = None
        for b in range(PACK):
            vx = PACK * q + b
            below, here, above = uext[vx], uext[vx + 1], uext[vx + 2]
            lower, upper = both_vy(here, hy[0, vx])
            grad_x = 0.5 * (above - below)
            grad_y = 0.5 * (upper - lower)
            laplace = above + below + upper + lower - 4.0 * here
            speed_x = jnp.abs(advect_rate * vx_hat(vx))
            moved = speed_x * (x_neighbour(here, 0, q, b, jnp.logical_not(high_x)) - here)
            moved = moved + speed_y * (y_neighbour(here, jnp.logical_not(high_y)) - here)
            new = here + moved - hamilton_rate * (grad_x * grad_x + grad_y * grad_y) + diffusion * laplace
            pre[vx] = new
            face = packed(face, new, b)
        send_packed(0, q, face, make_u)
        return 0

    lax.fori_loop(0, PACK, value_step, 0)

    arrive(g_vx)
    for s in range(2):
        gext[s] = jnp.where(i == 0, 0.0, gext[s])
        gext[BX + 2 + s] = jnp.where(i == KX - 1, 0.0, gext[BX + 2 + s])

    def grads_x(e, _):
        gradx[e] = 0.5 * (gext[e + 2] - gext[e])
        return 0

    lax.fori_loop(0, BX + 2, grads_x, 0)
    arrive(g_vy)

    def grads_y(vx, _):
        low = jnp.where(j == 0, 0.0, gvy[2, vx])
        high = jnp.where(j == KY - 1, 0.0, gvy[3, vx])
        slab = gext[vx + 2]
        edge = jnp.where(lo8, roll4(low), roll4(high))
        lower, upper = both_vy(slab, edge)
        grady[vx] = 0.5 * (upper - lower)
        gradh[vx] = jnp.where(lo8, 0.5 * (slab[0] - low), 0.5 * (high - slab[TILES - 1]))
        return 0

    lax.fori_loop(0, BX, grads_y, 0)

    vx_halo(mext, m_vx)
    vy_halo(2, m_vy)
    arrive([m_x])
    stats0 = depth_finish(0, depth0, False)

    def write_field(vx, slab):
        field[vx] = slab

    sums1, make_1 = forward(mext, 2, 1, stats0, write_field, 1)
    put_moments(20, sums1)
    plane1 = plane_start(1)

    def write_v(vx, slab):
        vext[vx + 1] = slab

    reflect(0, make_u, lambda vx: pre[vx], write_v)
    v_vx = vx_faces(vext)
    x_faces(2, lambda vx: vext[vx + 1], jnp.logical_not(high_x))
    v_x = x_send(2, jnp.logical_not(high_x))
    depth1 = plane_finish(1, plane1)

    def write_m(vx, slab):
        mext2[vx + 1] = slab

    reflect(1, make_1, lambda vx: field[vx], write_m)
    n_vx = vx_faces(mext2)
    n_vy = vy_faces(4, lambda vx, t: mext2[vx + 1, t])
    x_faces(3, lambda vx: mext2[vx + 1], high_x)
    n_x = x_send(3, high_x)

    arrive([v_x])
    make_z = mirror_copies(2)

    def transport_step(q, _):
        face = None
        for b in range(PACK):
            vx = PACK * q + b
            here = vext[vx + 1]
            speed_x = jnp.abs(advect_rate * vx_hat(vx))
            moved = speed_x * x_neighbour(here, 2, q, b, jnp.logical_not(high_x))
            moved = moved + speed_y * y_neighbour(here, jnp.logical_not(high_y))
            pre[vx] = moved
            face = packed(face, moved, b)
        send_packed(2, q, face, make_z)
        return 0

    lax.fori_loop(0, PACK, transport_step, 0)
    v_vy = vy_faces(6, lambda vx, t: vext[vx + 1, t])

    stats1 = depth_finish(1, depth1, True)
    vx_halo(mext2, n_vx)
    vy_halo(4, n_vy)
    arrive([n_x])

    def write_out(vx, slab):
        mo_ref[vx] = slab

    sums2, make_2 = forward(mext2, 4, 3, stats1, write_out, 3)
    put_moments(40, sums2)
    plane2 = plane_start(2)

    def write_z(vx, slab):
        wz[vx] = slab

    vx_halo(vext, v_vx)
    vy_halo(6, v_vy)
    depth2 = plane_finish(2, plane2)
    reflect(2, make_z, lambda vx: pre[vx], write_z)
    total2, mean_x2, mean_y2 = depth_finish(2, depth2, True)

    half = 0.5 * time_step * velocity_cost

    def coefficients(total, mean_x, mean_y):
        density = time_step * density_cost * (total / (VX * VY))
        return density + half * (mean_x * mean_x + mean_y * mean_y), 2.0 * half * mean_x, 2.0 * half * mean_y

    c0, c1, c2 = coefficients(total2, mean_x2, mean_y2)
    e0, e1, e2 = coefficients(*stats1)
    tiles[0] = c0
    tiles[1] = c1
    tiles[2] = c2
    back = jnp.logical_not(high_x)
    stats_peer = {"gx": jnp.where(back, (gx + 1) % gx_count, (gx + gx_count - 1) % gx_count)}
    stats_copy = start(tiles.at[pl.ds(0, 3)], tiles.at[pl.ds(3, 3)], stats_peer)

    def write_end(vx, slab):
        mo_ref[vx] = slab

    reflect(3, make_2, lambda vx: mo_ref[vx], write_end)
    arrive([stats_copy])

    def x_tile(t):
        here = tiles[t]
        shifted = jnp.where(back, pltpu.roll(here, 1, axis=0), pltpu.roll(here, 7, axis=0))
        far = jnp.where(back, pltpu.roll(tiles[3 + t], 5, axis=0), pltpu.roll(tiles[3 + t], 3, axis=0))
        return jnp.where(row % 4 == jnp.where(back, 0, 3), far, shifted)

    down_y = jnp.logical_not(high_y)
    near = jnp.where(down_y, 1, 127)
    away = jnp.where(down_y, 127, 1)
    y_near = [pltpu.roll(c, near, axis=1) for c in (c0, c1, c2)]
    y_away = [pltpu.roll(c, away, axis=1) for c in (c0, c1, c2)]
    x0, x1, x2 = x_tile(0), x_tile(1), jnp.where(wall, 0.0, x_tile(2))
    y0 = jnp.where(wall, 0.5 * (y_near[0] + y_away[0]), y_near[0])
    y1 = jnp.where(wall, 0.5 * (y_near[1] + y_away[1]), y_near[1])
    y2 = jnp.where(wall, 0.5 * (y_near[2] - y_away[2]), y_near[2])

    def cost(k0, k1, k2, vxh, vyh):
        return k0 - k1 * vxh - k2 * vyh + half * (vxh * vxh + vyh * vyh)

    def last_step(vx, _):
        vxh, vxh_low, vxh_high = vx_hat(vx), vx_hat(vx - 1), vx_hat(vx + 1)
        run_v = half * vy_hat * vy_hat - c2[None] * vy_hat + c0[None]
        run = (half * vxh * vxh - c1 * vxh)[None] + run_v
        has_low = (i * BX + vx) > 0
        has_high = (i * BX + vx) < VX - 1
        here = vext[vx + 1] + run
        below = vext[vx] + jnp.where(has_low, (half * vxh_low * vxh_low - c1 * vxh_low)[None] + run_v, 0.0)
        above = vext[vx + 2] + jnp.where(has_high, (half * vxh_high * vxh_high - c1 * vxh_high)[None] + run_v, 0.0)
        edge = hy[3, vx] + jnp.where(inside_edge, cost(c0, c1, c2, vxh, vy_hat_edge), 0.0)
        lower, upper = both_vy(here, edge)
        grad_x = 0.5 * (above - below)
        grad_y = 0.5 * (upper - lower)
        laplace = above + below + upper + lower - 4.0 * here
        speed_x = jnp.abs(advect_rate * vxh)
        moved = wz[vx] + speed_x * cost(x0[None], x1[None], x2[None], vxh, vy_hat)
        moved = moved + speed_y * cost(y0[None], y1[None], y2[None], vxh, vy_hat)
        moved = moved - (speed_x + speed_y) * here
        new = here + moved - hamilton_rate * (grad_x * grad_x + grad_y * grad_y) + diffusion * laplace
        vo_ref[vx] = new + cost(e0[None], e1[None], e2[None], vxh, vy_hat)
        return 0

    lax.fori_loop(0, BX, last_step, 0)

    for c in sent:
        c.wait_send()
    for make in (make_u, make_1, make_z, make_2):
        for q in range(PACK):
            make(q).wait_send()


def per_device(density_start, value_guess, value_end, walls):
    field_shape = (BX, TILES, 8, 128)

    def tiled(a):
        return a.reshape(field_shape)

    vmem = pl.BlockSpec(memory_space=pltpu.VMEM)

    def slabs(n):
        return pltpu.VMEM((n, TILES, 8, 128), F32)

    def stacks(n, m):
        return pltpu.VMEM((n, m, TILES, 8, 128), F32)

    out = jax.ShapeDtypeStruct(field_shape, F32)
    density_end, value_start = pl.pallas_call(
        kernel,
        out_shape=(out, out),
        in_specs=[vmem] * 4,
        out_specs=(vmem, vmem),
        scratch_shapes=[
            slabs(18), slabs(18), slabs(20), slabs(18), slabs(16),
            pltpu.VMEM((16, 8, 128), F32),
            slabs(18), slabs(18), slabs(16), slabs(18), slabs(18), slabs(16), slabs(16),
            pltpu.VMEM((4, 16, 8, 128), F32),
            stacks(4, 4),
            pltpu.VMEM((4, 8, 8, 128), F32), pltpu.VMEM((4, 8, 8, 128), F32),
            pltpu.VMEM((8, 8, 8, 128), F32),
            stacks(4, 4),
            pltpu.VMEM((4, 16, 8, 128), F32),
            stacks(4, 4), stacks(4, 4),
            pltpu.VMEM((60, 2, 8, 128), F32),
            pltpu.VMEM((6, 8, 128), F32),
            pltpu.VMEM((2, 8, 128), jnp.int32),
            pltpu.SemaphoreType.DMA((112,)),
            pltpu.SemaphoreType.DMA((112,)),
        ],
        compiler_params=pltpu.CompilerParams(
            collective_id=0, has_side_effects=True, vmem_limit_bytes=40 * 1024 * 1024
        ),
    )(tiled(density_start), tiled(value_guess), tiled(value_end), walls)
    return density_end.reshape(density_start.shape), value_start.reshape(density_start.shape)


def solution(mesh):
    return jax.shard_map(
        per_device,
        mesh=mesh,
        in_specs=(
            P("vert", None, None, "gx", None),
            P("vert", None, None, "gx", None),
            P("vert", None, None, "gx", None),
            P("gx", None),
        ),
        out_specs=(P("vert", None, None, "gx", None), P("vert", None, None, "gx", None)),
        check_vma=False,
    )
```

```python
import functools

import jax
import jax.numpy as jnp
from jax import lax
from jax.experimental import pallas as pl
from jax.experimental.pallas import tpu as pltpu
from jax.sharding import PartitionSpec as P

MESH = pl.DeviceIdType.MESH
F32 = jnp.float32

VX = 128
VY = 128
KX = 8
KY = 8
BX = 16
BY = 16
TILES = 8
EARLY = 3
PACK = 4

advect_rate = 0.3
diffusion = 0.05
drift_limit = 0.1
hamilton_rate = 0.05
time_step = 0.2
density_cost = 2.0
velocity_cost = 1.0


def roll4(a):
    return pltpu.roll(a, 4, axis=a.ndim - 2)


def kernel(
    m_hbm, g_hbm, u_hbm, walls_hbm, mo_ref, vo_ref,
    mext, mext2, gext, gradx, grady, gradh, upx, dnx, upy, dny, base, field, uext, vext, pre, wz,
    hy, xh, ylo, yhi, ysend, xsend, gvy, csend, crecv, red, idx, walls_ref,
    send_sem, recv_sem, load_sem,
):
    vert = lax.axis_index("vert")
    gx = lax.axis_index("gx")
    gx_count = lax.axis_size("gx")
    i = vert // KY
    j = vert % KY
    zh = vert % 4
    px = (vert // 4) % 4
    py = vert // 16

    def at(y, x, z):
        return {"vert": ((y % 4) * 4 + x % 4) * 4 + z % 4}

    plane = [at(py + d // 4, px + d % 4, zh) for d in range(1, 16)]
    depth = [at(py, px, zh + d) for d in range(1, 4)]
    mirror = {"vert": i * KY + (KY - 1 - j)}
    vx_up = {"vert": ((i + 1) % KX) * KY + j}
    vx_down = {"vert": ((i + KX - 1) % KX) * KY + j}
    vy_up = {"vert": i * KY + (j + 1) % KY}
    vy_down = {"vert": i * KY + (j + KY - 1) % KY}
    x_up = {"gx": (gx + 1) % gx_count}
    x_down = {"gx": (gx + gx_count - 1) % gx_count}

    loads = [
        pltpu.make_async_copy(m_hbm, mext.at[pl.ds(1, BX)], load_sem.at[0]),
        pltpu.make_async_copy(walls_hbm, walls_ref, load_sem.at[1]),
        pltpu.make_async_copy(u_hbm, uext.at[pl.ds(1, BX)], load_sem.at[2]),
        pltpu.make_async_copy(g_hbm, gext.at[pl.ds(2, BX)], load_sem.at[3]),
    ]
    for load in loads:
        load.start()

    barrier = pltpu.get_barrier_semaphore()
    roles = depth + [mirror, vy_up, vy_down] + plane + [x_up, x_down]
    for peer in roles:
        pl.semaphore_signal(barrier, inc=1, device_id=peer, device_id_type=MESH)

    row = lax.broadcasted_iota(jnp.int32, (8, 128), 0)
    lane = lax.broadcasted_iota(jnp.int32, (8, 128), 1)
    lo8 = row < 4
    high_x = i >= KX // 2
    high_y = j >= KY // 2

    def vx_hat(e):
        return ((i * BX + e).astype(F32) - (VX - 1) / 2.0) / (VX / 2.0)

    shape = (TILES, 8, 128)
    vy_row = 2 * lax.broadcasted_iota(jnp.int32, shape, 0) + lax.broadcasted_iota(jnp.int32, shape, 1) // 4
    vy_hat = ((j * BY + vy_row).astype(F32) - (VY - 1) / 2.0) / (VY / 2.0)
    vy_edge = jnp.where(lo8, j * BY - 1, j * BY + BY)
    vy_hat_edge = (vy_edge.astype(F32) - (VY - 1) / 2.0) / (VY / 2.0)
    inside_edge = (vy_edge >= 0) & (vy_edge < VY)
    speed_y = jnp.abs(advect_rate * vy_hat)

    def local_moments(read):
        def body(vx, carry):
            total, mom_x, mom_y = carry
            slab = read(vx)
            s = jnp.sum(slab, axis=0)
            return (total + s, mom_x + vx_hat(vx) * s, mom_y + jnp.sum(vy_hat * slab, axis=0))

        zero = jnp.zeros((8, 128), F32)
        return lax.fori_loop(0, BX, body, (zero, zero, zero))

    def put_moments(slot, sums, mom_y_cells=None):
        total, mom_x, mom_y = (a + roll4(a) for a in sums)
        if mom_y_cells is not None:
            mom_y = jnp.where(mom_y_cells, mom_y, 0.0)
        red[slot, 0] = jnp.where(lo8, total, mom_x)
        red[slot, 1] = mom_y

    loads[0].wait()
    put_moments(0, local_moments(lambda vx: mext[vx + 1]))

    loads[1].wait()
    w4 = walls_ref[...]
    wall = jnp.concatenate([w4, w4], axis=0) == 1
    ones = wall.astype(F32)
    sub128 = lax.broadcasted_iota(jnp.int32, (128, 128), 0)
    lane128 = lax.broadcasted_iota(jnp.int32, (128, 128), 1)
    upto = (sub128 <= lane128).astype(F32)
    count = jnp.dot(ones, upto, preferred_element_type=F32)
    count_t = lax.dot_general(
        (lane128 <= sub128).astype(F32), ones, (((1,), (1,)), ((), ())), preferred_element_type=F32
    )
    rank = jnp.clip(count.astype(jnp.int32) - 1, 0, 31)
    nth = (lane128 % 32).astype(F32)
    pick = jnp.zeros((8, 128), F32)
    for x in range(4):
        place = jnp.sum((count_t[:, x : x + 1] <= nth).astype(F32), axis=0, keepdims=True)
        pick = jnp.where(row % 4 == x, place, pick)
    idx[0] = jnp.minimum(pick.astype(jnp.int32), 127)
    idx[1] = rank

    def along_y(slab, index):
        return jnp.take_along_axis(slab, jnp.broadcast_to(index[None], shape), axis=2)


    counter = [0]

    def copy(src, dst, peer):
        n = counter[0]
        counter[0] += 1
        return pltpu.make_async_remote_copy(
            src_ref=src, dst_ref=dst, send_sem=send_sem.at[n], recv_sem=recv_sem.at[n],
            device_id=peer, device_id_type=MESH,
        )

    sent = []

    def start(src, dst, peer):
        c = copy(src, dst, peer)
        c.start()
        sent.append(c)
        return c

    def arrive(copies):
        for c in copies:
            c.wait_recv()

    def sums(r, slot):
        return red.at[slot] if r == 2 else red.at[slot, pl.ds(0, 2)]

    def depth_start(r, own=None):
        base = 20 * r
        own = base if own is None else own
        return [start(sums(r, own), sums(r, base + 1 + d), peer) for d, peer in enumerate(depth)]

    def plane_start(r, copies, own=None):
        base = 20 * r
        arrive(copies)
        tiles = 3 if r == 2 else 2
        acc = red[base if own is None else own, :tiles]
        for d in range(3):
            acc = acc + red[base + 1 + d, :tiles]
        red[base + 4, :tiles] = acc
        return [start(sums(r, base + 4), sums(r, base + 5 + d), peer) for d, peer in enumerate(plane)]

    def plane_finish(r, copies):
        base = 20 * r
        arrive(copies)
        tiles = 3 if r == 2 else 2
        acc = red[base + 4, :tiles]
        for d in range(15):
            acc = acc + red[base + 5 + d, :tiles]
        swapped = roll4(acc[0])
        total = jnp.where(lo8, acc[0], swapped)
        mom_x = jnp.where(lo8, swapped, acc[0])
        return (total, mom_x / total, acc[1] / total), acc[tiles - 1]

    def vy_pack(slot, read):
        def body(p, _):
            a0, a1 = read(2 * p, TILES - 1), read(2 * p + 1, TILES - 1)
            ysend[slot, p] = jnp.where(lo8, roll4(a0), a1)
            b0, b1 = read(2 * p, 0), read(2 * p + 1, 0)
            ysend[slot + 1, p] = jnp.where(lo8, b0, roll4(b1))
            return 0

        lax.fori_loop(0, BX // 2, body, 0)

    def vy_send(slot):
        return [
            start(ysend.at[slot], ylo.at[slot // 2], vy_up),
            start(ysend.at[slot + 1], yhi.at[slot // 2], vy_down),
        ]

    def vy_halo(slot, copies):
        arrive(copies)

        def body(p, _):
            low, high = ylo[slot // 2, p], yhi[slot // 2, p]
            hy[slot // 2, 2 * p] = jnp.where(inside_edge, jnp.where(lo8, low, roll4(high)), 0.0)
            hy[slot // 2, 2 * p + 1] = jnp.where(inside_edge, jnp.where(lo8, roll4(low), high), 0.0)
            return 0

        lax.fori_loop(0, BX // 2, body, 0)

    def vx_faces(ext):
        return [
            start(ext.at[BX], ext.at[0], vx_up),
            start(ext.at[1], ext.at[BX + 1], vx_down),
        ]

    def vx_halo(ext, copies):
        arrive(copies)
        ext[0] = jnp.where(i == 0, 0.0, ext[0])
        ext[BX + 1] = jnp.where(i == KX - 1, 0.0, ext[BX + 1])

    def x_pack(slot, read, below):
        def body(q, _):
            face = None
            for b in range(PACK):
                slab = read(PACK * q + b)
                moved = jnp.where(below, pltpu.roll(slab, (b - 3) % 8, axis=1), pltpu.roll(slab, (b + 3) % 8, axis=1))
                target = jnp.where(below, b, b + 3) % 4
                face = moved if face is None else jnp.where((row % 4 == target)[None], moved, face)
            xsend[slot, q] = face
            return 0

        lax.fori_loop(0, BX // PACK, body, 0)

    def x_neighbour(slab, slot, q, b, below):
        shifted = jnp.where(below, pltpu.roll(slab, 1, axis=1), pltpu.roll(slab, 7, axis=1))
        edge = row % 4 == jnp.where(below, 0, 3)
        return jnp.where(edge[None], pltpu.roll(xh[slot, q], (8 - b) % 8, axis=1), shifted)

    def y_neighbour(slab, below):
        return pltpu.roll(slab, jnp.where(below, 1, 127), axis=2)

    def vy_neighbours(low, high, edge_low, edge_high):
        r_low, r_high = roll4(low), roll4(high)
        lower = jnp.where(lo8[None], jnp.concatenate([edge_low[None], r_low[:-1]], axis=0), r_low)
        upper = jnp.where(lo8[None], r_high, jnp.concatenate([r_high[1:], edge_high[None]], axis=0))
        return lower, upper

    def both_vy(slab, edge):
        r = roll4(slab)
        lower = jnp.where(lo8[None], jnp.concatenate([edge[None], r[:-1]], axis=0), r)
        upper = jnp.where(lo8[None], r, jnp.concatenate([r[1:], edge[None]], axis=0))
        return lower, upper

    def x_send(slot, below):
        peer = {"gx": jnp.where(below, (gx + 1) % gx_count, (gx + gx_count - 1) % gx_count)}
        return start(xsend.at[slot], xh.at[slot], peer)

    def mirror_copies(slot):
        n = counter[0]
        counter[0] += PACK

        def make(q):
            return pltpu.make_async_remote_copy(
                src_ref=csend.at[slot, q], dst_ref=crecv.at[slot, q],
                send_sem=send_sem.at[n + q], recv_sem=recv_sem.at[n + q],
                device_id=mirror, device_id_type=MESH,
            )

        return make

    def packed(face, slab, b):
        taken = along_y(slab, idx[0])
        return taken if face is None else jnp.where((lane // 32 == b)[None], taken, face)

    def turn(slot, q, face):
        turned = roll4(face)
        for t in range(TILES):
            csend[slot, q, t] = turned[TILES - 1 - t]

    def reflect(slot, make, read, write):
        def body(q, carry):
            make(q).wait_recv()
            face = crecv[slot, q]
            for b in range(PACK):
                vx = PACK * q + b
                slab = read(vx)
                other = along_y(face, idx[1] + 32 * b)
                write(vx, jnp.where(wall[None], 0.5 * (slab + other), slab))
            return carry

        lax.fori_loop(0, PACK, body, 0)

    def x_rates(ext, e, mean_x):
        cells = ext[e]
        drift = drift_limit * jnp.tanh((mean_x - vx_hat(e - 1))[None] - gradx[e])
        upx[e] = cells * (diffusion + jnp.maximum(drift, 0.0))
        dnx[e] = cells * (diffusion + jnp.maximum(-drift, 0.0))

    def outflow(ext, stats):
        total, mean_x, mean_y = stats

        def body(vx, _):
            x_rates(ext, vx + 1, mean_x)
            cells = ext[vx + 1]
            drift = drift_limit * jnp.tanh(mean_y[None] - vy_hat - grady[vx])
            upy[vx] = cells * (diffusion + jnp.maximum(drift, 0.0))
            dny[vx] = cells * (diffusion + jnp.maximum(-drift, 0.0))
            return 0

        lax.fori_loop(0, BX, body, 0)

    def stay(ext, xslot):
        step_x, step_y = 2.0 / VX, 2.0 / VY
        top_y = jnp.where(jnp.logical_and(j == KY - 1, row >= 4), 1.0, 0.0)
        bottom_y = jnp.where(jnp.logical_and(j == 0, row < 4), 1.0, 0.0)

        def body(q, carry):
            total, mom_x, mom_y = carry
            for b in range(PACK):
                vx = PACK * q + b
                cells = ext[vx + 1]
                up_x, down_x, up_y, down_y = upx[vx + 1], dnx[vx + 1], upy[vx], dny[vx]
                speed_x = jnp.abs(advect_rate * vx_hat(vx))
                moved = speed_x * (cells - x_neighbour(cells, xslot, q, b, high_x))
                moved = moved + speed_y * (cells - y_neighbour(cells, high_y))
                kept = cells - moved
                base[vx] = kept - (up_x + down_x + up_y + down_y)
                s = jnp.sum(kept, axis=0)
                lost_up, lost_down = top_y * up_y[TILES - 1], bottom_y * down_y[0]
                total = total + s - (lost_up + lost_down)
                mom_x = mom_x + vx_hat(vx) * (s - (lost_up + lost_down)) + step_x * jnp.sum(up_x - down_x, axis=0)
                mom_y = mom_y + jnp.sum(vy_hat * kept + step_y * (up_y - down_y), axis=0)
                mom_y = mom_y - vy_hat_edge * (lost_up + lost_down)
            return total, mom_x, mom_y

        zero = jnp.zeros((8, 128), F32)
        total, mom_x, mom_y = lax.fori_loop(0, PACK, body, (zero, zero, zero))
        lost_up = jnp.where(i == KX - 1, 1.0, 0.0) * upx[BX]
        lost_down = jnp.where(i == 0, 1.0, 0.0) * dnx[1]
        s_up, s_down = jnp.sum(lost_up, axis=0), jnp.sum(lost_down, axis=0)
        total = total - (s_up + s_down)
        mom_x = mom_x - vx_hat(jnp.int32(BX)) * s_up - vx_hat(jnp.int32(-1)) * s_down
        mom_y = mom_y - jnp.sum(vy_hat * (lost_up + lost_down), axis=0)
        return total, mom_x, mom_y

    def inflow(ext, hslot, stats, write, cslot):
        total, mean_x, mean_y = stats
        x_rates(ext, 0, mean_x)
        x_rates(ext, BX + 1, mean_x)

        def body(q, _):
            face = None
            for b in range(PACK):
                vx = PACK * q + b
                drift = drift_limit * jnp.tanh(mean_y - vy_hat_edge - gradh[vx])
                cells = hy[hslot, vx]
                up_edge = cells * (diffusion + jnp.maximum(drift, 0.0))
                down_edge = cells * (diffusion + jnp.maximum(-drift, 0.0))
                lower, upper = vy_neighbours(upy[vx], dny[vx], up_edge, down_edge)
                new = base[vx] + upx[vx] + dnx[vx + 2] + lower + upper
                write(vx, new)
                face = packed(face, new, b)
            turn(cslot, q, face)
            return 0

        lax.fori_loop(0, PACK, body, 0)

    vy_pack(2, lambda vx, t: mext[vx + 1, t])
    x_pack(1, lambda vx: mext[vx + 1], high_x)
    loads[2].wait()
    vy_pack(0, lambda vx, t: uext[vx + 1, t])
    x_pack(0, lambda vx: uext[vx + 1], jnp.logical_not(high_x))
    loads[3].wait()

    def fill_g(vx, _):
        gvy[0, vx] = gext[vx + 2, TILES - 1]
        gvy[1, vx] = gext[vx + 2, 0]
        return 0

    lax.fori_loop(0, BX, fill_g, 0)
    pl.semaphore_wait(barrier, len(roles))

    depth0 = depth_start(0)
    u_vy = vy_send(0)
    u_vx = vx_faces(uext)
    u_x = x_send(0, jnp.logical_not(high_x))
    m_vy = vy_send(2)
    g_vy = [start(gvy.at[0], gvy.at[2], vy_up), start(gvy.at[1], gvy.at[3], vy_down)]
    m_vx = vx_faces(mext)
    g_vx = [
        start(gext.at[pl.ds(BX, 2)], gext.at[pl.ds(0, 2)], vx_up),
        start(gext.at[pl.ds(2, 2)], gext.at[pl.ds(BX + 2, 2)], vx_down),
    ]
    m_x = x_send(1, high_x)
    plane0 = plane_start(0, depth0)

    vx_halo(uext, u_vx)
    vy_halo(0, u_vy)
    arrive([u_x])
    make_u = mirror_copies(0)

    def value_step(q, _):
        face = None
        for b in range(PACK):
            vx = PACK * q + b
            below, here, above = uext[vx], uext[vx + 1], uext[vx + 2]
            lower, upper = both_vy(here, hy[0, vx])
            grad_x = 0.5 * (above - below)
            grad_y = 0.5 * (upper - lower)
            laplace = above + below + upper + lower - 4.0 * here
            speed_x = jnp.abs(advect_rate * vx_hat(vx))
            moved = speed_x * (x_neighbour(here, 0, q, b, jnp.logical_not(high_x)) - here)
            moved = moved + speed_y * (y_neighbour(here, jnp.logical_not(high_y)) - here)
            new = here + moved - hamilton_rate * (grad_x * grad_x + grad_y * grad_y) + diffusion * laplace
            pre[vx] = new
            face = packed(face, new, b)
        turn(0, q, face)
        make_u(q).start()
        return 0

    lax.fori_loop(0, PACK, value_step, 0)

    arrive(g_vx)
    for s in range(2):
        gext[s] = jnp.where(i == 0, 0.0, gext[s])
        gext[BX + 2 + s] = jnp.where(i == KX - 1, 0.0, gext[BX + 2 + s])

    def grads_x(e, _):
        gradx[e] = 0.5 * (gext[e + 2] - gext[e])
        return 0

    lax.fori_loop(0, BX + 2, grads_x, 0)
    arrive(g_vy)

    def grads_y(vx, _):
        low = jnp.where(j == 0, 0.0, gvy[2, vx])
        high = jnp.where(j == KY - 1, 0.0, gvy[3, vx])
        slab = gext[vx + 2]
        edge = jnp.where(lo8, roll4(low), roll4(high))
        lower, upper = both_vy(slab, edge)
        grady[vx] = 0.5 * (upper - lower)
        gradh[vx] = jnp.where(lo8, 0.5 * (slab[0] - low), 0.5 * (high - slab[TILES - 1]))
        return 0

    lax.fori_loop(0, BX, grads_y, 0)

    vx_halo(mext, m_vx)
    vy_halo(2, m_vy)
    arrive([m_x])
    stats0, _ = plane_finish(0, plane0)
    outflow(mext, stats0)
    put_moments(20, stay(mext, 1), jnp.logical_not(wall))
    depth1 = depth_start(1)

    def write_field(vx, slab):
        field[vx] = slab

    inflow(mext, 1, stats0, write_field, 1)
    make_1 = mirror_copies(1)
    for q in range(EARLY):
        make_1(q).start()

    def write_v(vx, slab):
        vext[vx + 1] = slab

    plane1 = plane_start(1, depth1)
    for q in range(EARLY, PACK):
        make_1(q).start()
    reflect(0, make_u, lambda vx: pre[vx], write_v)
    x_pack(2, lambda vx: vext[vx + 1], jnp.logical_not(high_x))
    v_x = x_send(2, jnp.logical_not(high_x))
    v_vx = vx_faces(vext)
    vy_pack(6, lambda vx, t: vext[vx + 1, t])
    v_vy = vy_send(6)

    arrive([v_x])
    make_z = mirror_copies(2)

    def transport_step(q, _):
        face = None
        for b in range(PACK):
            vx = PACK * q + b
            here = vext[vx + 1]
            speed_x = jnp.abs(advect_rate * vx_hat(vx))
            moved = speed_x * x_neighbour(here, 2, q, b, jnp.logical_not(high_x))
            moved = moved + speed_y * y_neighbour(here, jnp.logical_not(high_y))
            pre[vx] = moved
            face = packed(face, moved, b)
        turn(2, q, face)
        return 0

    lax.fori_loop(0, PACK, transport_step, 0)
    for q in range(PACK):
        make_z(q).start()

    def write_m(vx, slab):
        mext2[vx + 1] = slab

    reflect(1, make_1, lambda vx: field[vx], write_m)
    vy_pack(4, lambda vx, t: mext2[vx + 1, t])
    n_vy = vy_send(4)
    n_vx = vx_faces(mext2)
    x_pack(3, lambda vx: mext2[vx + 1], high_x)
    n_x = x_send(3, high_x)

    stats1, _ = plane_finish(1, plane1)
    outflow(mext2, stats1)
    arrive([n_x])
    put_moments(40, stay(mext2, 3), jnp.logical_not(wall))
    arrive([start(sums(0, 40), sums(0, 60), x_up), start(sums(0, 40), sums(0, 61), x_down)])
    third = jnp.zeros((8, 128), F32)
    for k, (t, r) in enumerate(((0, 0), (0, 4), (1, 0))):
        third = jnp.where(row == k, red[60, t, r + 3 : r + 4], third)
        third = jnp.where(row == 3 + k, red[61, t, r : r + 1], third)
    red[62, 0] = red[40, 0]
    red[62, 1] = red[40, 1]
    red[62, 2] = third
    depth2 = depth_start(2, 62)
    vx_halo(mext2, n_vx)
    vy_halo(4, n_vy)

    def write_out(vx, slab):
        mo_ref[vx] = slab

    inflow(mext2, 2, stats1, write_out, 3)
    make_2 = mirror_copies(3)
    for q in range(EARLY):
        make_2(q).start()

    def write_z(vx, slab):
        wz[vx] = slab

    vx_halo(vext, v_vx)
    vy_halo(6, v_vy)
    plane2 = plane_start(2, depth2, 62)
    for q in range(EARLY, PACK):
        make_2(q).start()
    reflect(2, make_z, lambda vx: pre[vx], write_z)
    (total2, mean_x2, mean_y2), near = plane_finish(2, plane2)

    half = 0.5 * time_step * velocity_cost

    def coefficients(total, mean_x, mean_y):
        density = time_step * density_cost * (total / (VX * VY))
        return density + half * (mean_x * mean_x + mean_y * mean_y), 2.0 * half * mean_x, 2.0 * half * mean_y

    c0, c1, c2 = coefficients(total2, mean_x2, mean_y2)
    e0, e1, e2 = coefficients(*stats1)
    back = jnp.logical_not(high_x)
    edge_row = row % 4 == jnp.where(back, 0, 3)

    near_sums = [jnp.where(back, near[k : k + 1], near[3 + k : 4 + k]) for k in range(3)]
    near_coefficients = coefficients(near_sums[0], near_sums[1] / near_sums[0], near_sums[2] / near_sums[0])

    def x_tile(here, far):
        shifted = jnp.where(back, pltpu.roll(here, 1, axis=0), pltpu.roll(here, 7, axis=0))
        return jnp.where(edge_row, far, shifted)

    down_y = jnp.logical_not(high_y)
    near = jnp.where(down_y, 1, 127)
    away = jnp.where(down_y, 127, 1)
    y_near = [pltpu.roll(c, near, axis=1) for c in (c0, c1, c2)]
    y_away = [pltpu.roll(c, away, axis=1) for c in (c0, c1, c2)]
    x0, x1, x2 = (x_tile(here, far) for here, far in zip((c0, c1, c2), near_coefficients))
    x2 = jnp.where(wall, 0.0, x2)
    y0 = jnp.where(wall, 0.5 * (y_near[0] + y_away[0]), y_near[0])
    y1 = jnp.where(wall, 0.5 * (y_near[1] + y_away[1]), y_near[1])
    y2 = jnp.where(wall, 0.5 * (y_near[2] - y_away[2]), y_near[2])

    def cost(k0, k1, k2, vxh, vyh):
        return k0 - k1 * vxh - k2 * vyh + half * (vxh * vxh + vyh * vyh)

    def last_step(vx, _):
        vxh, vxh_low, vxh_high = vx_hat(vx), vx_hat(vx - 1), vx_hat(vx + 1)
        run_v = half * vy_hat * vy_hat - c2[None] * vy_hat + c0[None]
        run = (half * vxh * vxh - c1 * vxh)[None] + run_v
        has_low = (i * BX + vx) > 0
        has_high = (i * BX + vx) < VX - 1
        here = vext[vx + 1] + run
        below = vext[vx] + jnp.where(has_low, (half * vxh_low * vxh_low - c1 * vxh_low)[None] + run_v, 0.0)
        above = vext[vx + 2] + jnp.where(has_high, (half * vxh_high * vxh_high - c1 * vxh_high)[None] + run_v, 0.0)
        edge = hy[3, vx] + jnp.where(inside_edge, cost(c0, c1, c2, vxh, vy_hat_edge), 0.0)
        lower, upper = both_vy(here, edge)
        grad_x = 0.5 * (above - below)
        grad_y = 0.5 * (upper - lower)
        laplace = above + below + upper + lower - 4.0 * here
        speed_x = jnp.abs(advect_rate * vxh)
        moved = wz[vx] + speed_x * cost(x0[None], x1[None], x2[None], vxh, vy_hat)
        moved = moved + speed_y * cost(y0[None], y1[None], y2[None], vxh, vy_hat)
        moved = moved - (speed_x + speed_y) * here
        new = here + moved - hamilton_rate * (grad_x * grad_x + grad_y * grad_y) + diffusion * laplace
        vo_ref[vx] = new + cost(e0[None], e1[None], e2[None], vxh, vy_hat)
        return 0

    lax.fori_loop(0, BX, last_step, 0)

    def write_end(vx, slab):
        mo_ref[vx] = slab

    reflect(3, make_2, lambda vx: mo_ref[vx], write_end)

    for c in sent:
        c.wait_send()
    for make in (make_u, make_1, make_z, make_2):
        for q in range(PACK):
            make(q).wait_send()


def per_device(density_start, value_guess, value_end, walls):
    field_shape = (BX, TILES, 8, 128)

    def tiled(a):
        return a.reshape(field_shape)

    vmem = pl.BlockSpec(memory_space=pltpu.VMEM)

    def slabs(n):
        return pltpu.VMEM((n, TILES, 8, 128), F32)

    def stacks(n, m):
        return pltpu.VMEM((n, m, TILES, 8, 128), F32)

    out = jax.ShapeDtypeStruct(field_shape, F32)
    density_end, value_start = pl.pallas_call(
        kernel,
        out_shape=(out, out),
        in_specs=[pl.BlockSpec(memory_space=pltpu.HBM)] * 4,
        out_specs=(vmem, vmem),
        scratch_shapes=[
            slabs(18), slabs(18), slabs(20), slabs(18), slabs(16),
            pltpu.VMEM((16, 8, 128), F32),
            slabs(18), slabs(18), slabs(16), slabs(16), slabs(16),
            slabs(16), slabs(18), slabs(18), slabs(16), slabs(16),
            pltpu.VMEM((4, 16, 8, 128), F32),
            stacks(4, 4),
            pltpu.VMEM((4, 8, 8, 128), F32), pltpu.VMEM((4, 8, 8, 128), F32),
            pltpu.VMEM((8, 8, 8, 128), F32),
            stacks(4, 4),
            pltpu.VMEM((4, 16, 8, 128), F32),
            stacks(4, 4), stacks(4, 4),
            pltpu.VMEM((63, 3, 8, 128), F32),
            pltpu.VMEM((2, 8, 128), jnp.int32),
            pltpu.VMEM((4, 128), jnp.int32),
            pltpu.SemaphoreType.DMA((112,)),
            pltpu.SemaphoreType.DMA((112,)),
            pltpu.SemaphoreType.DMA((4,)),
        ],
        compiler_params=pltpu.CompilerParams(
            collective_id=0, has_side_effects=True, vmem_limit_bytes=60 * 1024 * 1024
        ),
    )(tiled(density_start), tiled(value_guess), tiled(value_end), walls)
    return density_end.reshape(density_start.shape), value_start.reshape(density_start.shape)


def solution(mesh):
    return jax.shard_map(
        per_device,
        mesh=mesh,
        in_specs=(
            P("vert", None, None, "gx", None),
            P("vert", None, None, "gx", None),
            P("vert", None, None, "gx", None),
            P("gx", None),
        ),
        out_specs=(P("vert", None, None, "gx", None), P("vert", None, None, "gx", None)),
        check_vma=False,
    )
```

```python
import functools

import jax
import jax.numpy as jnp
from jax import lax
from jax.experimental import pallas as pl
from jax.experimental.pallas import tpu as pltpu
from jax.sharding import PartitionSpec as P

MESH = pl.DeviceIdType.MESH
F32 = jnp.float32

VX = 128
VY = 128
KX = 8
KY = 8
BX = 16
BY = 16
TILES = 8
EARLY = (3, 1)
PACK = 4

advect_rate = 0.3
diffusion = 0.05
drift_limit = 0.1
hamilton_rate = 0.05
time_step = 0.2
density_cost = 2.0
velocity_cost = 1.0


def roll4(a):
    return pltpu.roll(a, 4, axis=a.ndim - 2)


def kernel(
    m_hbm, g_hbm, u_hbm, walls_hbm, mo_ref, vo_ref,
    mext, mext2, gext, gradx, grady, gradh, upx, dnx, upy, dny, base, field, uext, vext, pre, wz,
    hy, xh, ylo, yhi, ysend, xsend, gvy, csend, crecv, red, tiles, idx, walls_ref,
    send_sem, recv_sem, load_sem,
):
    vert = lax.axis_index("vert")
    gx = lax.axis_index("gx")
    gx_count = lax.axis_size("gx")
    i = vert // KY
    j = vert % KY
    zh = vert % 4
    px = (vert // 4) % 4
    py = vert // 16

    def at(y, x, z):
        return {"vert": ((y % 4) * 4 + x % 4) * 4 + z % 4}

    plane = [at(py + d // 4, px + d % 4, zh) for d in range(1, 16)]
    depth = [at(py, px, zh + d) for d in range(1, 4)]
    mirror = {"vert": i * KY + (KY - 1 - j)}
    vx_up = {"vert": ((i + 1) % KX) * KY + j}
    vx_down = {"vert": ((i + KX - 1) % KX) * KY + j}
    vy_up = {"vert": i * KY + (j + 1) % KY}
    vy_down = {"vert": i * KY + (j + KY - 1) % KY}
    x_up = {"gx": (gx + 1) % gx_count}
    x_down = {"gx": (gx + gx_count - 1) % gx_count}

    loads = [
        pltpu.make_async_copy(m_hbm, mext.at[pl.ds(1, BX)], load_sem.at[0]),
        pltpu.make_async_copy(walls_hbm, walls_ref, load_sem.at[1]),
        pltpu.make_async_copy(u_hbm, uext.at[pl.ds(1, BX)], load_sem.at[2]),
        pltpu.make_async_copy(g_hbm, gext.at[pl.ds(2, BX)], load_sem.at[3]),
    ]
    for load in loads:
        load.start()

    barrier = pltpu.get_barrier_semaphore()
    roles = depth + [mirror, vy_up, vy_down] + plane + [x_up, x_down]
    for peer in roles:
        pl.semaphore_signal(barrier, inc=1, device_id=peer, device_id_type=MESH)

    row = lax.broadcasted_iota(jnp.int32, (8, 128), 0)
    lane = lax.broadcasted_iota(jnp.int32, (8, 128), 1)
    lo8 = row < 4
    high_x = i >= KX // 2
    high_y = j >= KY // 2

    def vx_hat(e):
        return ((i * BX + e).astype(F32) - (VX - 1) / 2.0) / (VX / 2.0)

    shape = (TILES, 8, 128)
    vy_row = 2 * lax.broadcasted_iota(jnp.int32, shape, 0) + lax.broadcasted_iota(jnp.int32, shape, 1) // 4
    vy_hat = ((j * BY + vy_row).astype(F32) - (VY - 1) / 2.0) / (VY / 2.0)
    vy_edge = jnp.where(lo8, j * BY - 1, j * BY + BY)
    vy_hat_edge = (vy_edge.astype(F32) - (VY - 1) / 2.0) / (VY / 2.0)
    inside_edge = (vy_edge >= 0) & (vy_edge < VY)
    speed_y = jnp.abs(advect_rate * vy_hat)

    def local_moments(read):
        def body(vx, carry):
            total, mom_x, mom_y = carry
            slab = read(vx)
            s = jnp.sum(slab, axis=0)
            return (total + s, mom_x + vx_hat(vx) * s, mom_y + jnp.sum(vy_hat * slab, axis=0))

        zero = jnp.zeros((8, 128), F32)
        return lax.fori_loop(0, BX, body, (zero, zero, zero))

    def put_moments(slot, sums, mom_y_cells=None):
        total, mom_x, mom_y = (a + roll4(a) for a in sums)
        if mom_y_cells is not None:
            mom_y = jnp.where(mom_y_cells, mom_y, 0.0)
        red[slot, 0] = jnp.where(lo8, total, mom_x)
        red[slot, 1] = mom_y

    loads[0].wait()
    put_moments(0, local_moments(lambda vx: mext[vx + 1]))

    loads[1].wait()
    w4 = walls_ref[...]
    wall = jnp.concatenate([w4, w4], axis=0) == 1
    ones = wall.astype(F32)
    sub128 = lax.broadcasted_iota(jnp.int32, (128, 128), 0)
    lane128 = lax.broadcasted_iota(jnp.int32, (128, 128), 1)
    upto = (sub128 <= lane128).astype(F32)
    count = jnp.dot(ones, upto, preferred_element_type=F32)
    count_t = lax.dot_general(
        (lane128 <= sub128).astype(F32), ones, (((1,), (1,)), ((), ())), preferred_element_type=F32
    )
    rank = jnp.clip(count.astype(jnp.int32) - 1, 0, 31)
    nth = (lane128 % 32).astype(F32)
    pick = jnp.zeros((8, 128), F32)
    for x in range(4):
        place = jnp.sum((count_t[:, x : x + 1] <= nth).astype(F32), axis=0, keepdims=True)
        pick = jnp.where(row % 4 == x, place, pick)
    idx[0] = jnp.minimum(pick.astype(jnp.int32), 127)
    idx[1] = rank

    def along_y(slab, index):
        return jnp.take_along_axis(slab, jnp.broadcast_to(index[None], shape), axis=2)


    counter = [0]

    def copy(src, dst, peer):
        n = counter[0]
        counter[0] += 1
        return pltpu.make_async_remote_copy(
            src_ref=src, dst_ref=dst, send_sem=send_sem.at[n], recv_sem=recv_sem.at[n],
            device_id=peer, device_id_type=MESH,
        )

    sent = []

    def start(src, dst, peer):
        c = copy(src, dst, peer)
        c.start()
        sent.append(c)
        return c

    def arrive(copies):
        for c in copies:
            c.wait_recv()

    def depth_start(r):
        base = 20 * r
        return [start(red.at[base], red.at[base + 1 + d], peer) for d, peer in enumerate(depth)]

    def plane_start(r, copies):
        base = 20 * r
        arrive(copies)
        acc = red[base]
        for d in range(3):
            acc = acc + red[base + 1 + d]
        red[base + 4] = acc
        return [start(red.at[base + 4], red.at[base + 5 + d], peer) for d, peer in enumerate(plane)]

    def plane_finish(r, copies):
        base = 20 * r
        arrive(copies)
        acc = red[base + 4]
        for d in range(15):
            acc = acc + red[base + 5 + d]
        swapped = roll4(acc[0])
        total = jnp.where(lo8, acc[0], swapped)
        mom_x = jnp.where(lo8, swapped, acc[0])
        return total, mom_x / total, acc[1] / total

    def vy_pack(slot, read):
        def body(p, _):
            a0, a1 = read(2 * p, TILES - 1), read(2 * p + 1, TILES - 1)
            ysend[slot, p] = jnp.where(lo8, roll4(a0), a1)
            b0, b1 = read(2 * p, 0), read(2 * p + 1, 0)
            ysend[slot + 1, p] = jnp.where(lo8, b0, roll4(b1))
            return 0

        lax.fori_loop(0, BX // 2, body, 0)

    def vy_send(slot):
        return [
            start(ysend.at[slot], ylo.at[slot // 2], vy_up),
            start(ysend.at[slot + 1], yhi.at[slot // 2], vy_down),
        ]

    def vy_halo(slot, copies):
        arrive(copies)

        def body(p, _):
            low, high = ylo[slot // 2, p], yhi[slot // 2, p]
            hy[slot // 2, 2 * p] = jnp.where(inside_edge, jnp.where(lo8, low, roll4(high)), 0.0)
            hy[slot // 2, 2 * p + 1] = jnp.where(inside_edge, jnp.where(lo8, roll4(low), high), 0.0)
            return 0

        lax.fori_loop(0, BX // 2, body, 0)

    def vx_faces(ext):
        return [
            start(ext.at[BX], ext.at[0], vx_up),
            start(ext.at[1], ext.at[BX + 1], vx_down),
        ]

    def vx_halo(ext, copies):
        arrive(copies)
        ext[0] = jnp.where(i == 0, 0.0, ext[0])
        ext[BX + 1] = jnp.where(i == KX - 1, 0.0, ext[BX + 1])

    def x_pack(slot, read, below):
        def body(q, _):
            face = None
            for b in range(PACK):
                slab = read(PACK * q + b)
                moved = jnp.where(below, pltpu.roll(slab, (b - 3) % 8, axis=1), pltpu.roll(slab, (b + 3) % 8, axis=1))
                target = jnp.where(below, b, b + 3) % 4
                face = moved if face is None else jnp.where((row % 4 == target)[None], moved, face)
            xsend[slot, q] = face
            return 0

        lax.fori_loop(0, BX // PACK, body, 0)

    def x_neighbour(slab, slot, q, b, below):
        shifted = jnp.where(below, pltpu.roll(slab, 1, axis=1), pltpu.roll(slab, 7, axis=1))
        edge = row % 4 == jnp.where(below, 0, 3)
        return jnp.where(edge[None], pltpu.roll(xh[slot, q], (8 - b) % 8, axis=1), shifted)

    def y_neighbour(slab, below):
        return pltpu.roll(slab, jnp.where(below, 1, 127), axis=2)

    def vy_neighbours(low, high, edge_low, edge_high):
        r_low, r_high = roll4(low), roll4(high)
        lower = jnp.where(lo8[None], jnp.concatenate([edge_low[None], r_low[:-1]], axis=0), r_low)
        upper = jnp.where(lo8[None], r_high, jnp.concatenate([r_high[1:], edge_high[None]], axis=0))
        return lower, upper

    def both_vy(slab, edge):
        r = roll4(slab)
        lower = jnp.where(lo8[None], jnp.concatenate([edge[None], r[:-1]], axis=0), r)
        upper = jnp.where(lo8[None], r, jnp.concatenate([r[1:], edge[None]], axis=0))
        return lower, upper

    def x_send(slot, below):
        peer = {"gx": jnp.where(below, (gx + 1) % gx_count, (gx + gx_count - 1) % gx_count)}
        return start(xsend.at[slot], xh.at[slot], peer)

    def mirror_copies(slot):
        n = counter[0]
        counter[0] += PACK

        def make(q):
            return pltpu.make_async_remote_copy(
                src_ref=csend.at[slot, q], dst_ref=crecv.at[slot, q],
                send_sem=send_sem.at[n + q], recv_sem=recv_sem.at[n + q],
                device_id=mirror, device_id_type=MESH,
            )

        return make

    def packed(face, slab, b):
        taken = along_y(slab, idx[0])
        return taken if face is None else jnp.where((lane // 32 == b)[None], taken, face)

    def turn(slot, q, face):
        turned = roll4(face)
        for t in range(TILES):
            csend[slot, q, t] = turned[TILES - 1 - t]

    def reflect(slot, make, read, write):
        def body(q, carry):
            make(q).wait_recv()
            face = crecv[slot, q]
            for b in range(PACK):
                vx = PACK * q + b
                slab = read(vx)
                other = along_y(face, idx[1] + 32 * b)
                write(vx, jnp.where(wall[None], 0.5 * (slab + other), slab))
            return carry

        lax.fori_loop(0, PACK, body, 0)

    def x_rates(ext, e, mean_x):
        cells = ext[e]
        drift = drift_limit * jnp.tanh((mean_x - vx_hat(e - 1))[None] - gradx[e])
        upx[e] = cells * (diffusion + jnp.maximum(drift, 0.0))
        dnx[e] = cells * (diffusion + jnp.maximum(-drift, 0.0))

    def outflow(ext, stats):
        total, mean_x, mean_y = stats

        def body(vx, _):
            x_rates(ext, vx + 1, mean_x)
            cells = ext[vx + 1]
            drift = drift_limit * jnp.tanh(mean_y[None] - vy_hat - grady[vx])
            upy[vx] = cells * (diffusion + jnp.maximum(drift, 0.0))
            dny[vx] = cells * (diffusion + jnp.maximum(-drift, 0.0))
            return 0

        lax.fori_loop(0, BX, body, 0)

    def stay(ext, xslot):
        step_x, step_y = 2.0 / VX, 2.0 / VY
        top_y = jnp.where(jnp.logical_and(j == KY - 1, row >= 4), 1.0, 0.0)
        bottom_y = jnp.where(jnp.logical_and(j == 0, row < 4), 1.0, 0.0)

        def body(q, carry):
            total, mom_x, mom_y = carry
            for b in range(PACK):
                vx = PACK * q + b
                cells = ext[vx + 1]
                up_x, down_x, up_y, down_y = upx[vx + 1], dnx[vx + 1], upy[vx], dny[vx]
                speed_x = jnp.abs(advect_rate * vx_hat(vx))
                moved = speed_x * (cells - x_neighbour(cells, xslot, q, b, high_x))
                moved = moved + speed_y * (cells - y_neighbour(cells, high_y))
                kept = cells - moved
                base[vx] = kept - (up_x + down_x + up_y + down_y)
                s = jnp.sum(kept, axis=0)
                lost_up, lost_down = top_y * up_y[TILES - 1], bottom_y * down_y[0]
                total = total + s - (lost_up + lost_down)
                mom_x = mom_x + vx_hat(vx) * (s - (lost_up + lost_down)) + step_x * jnp.sum(up_x - down_x, axis=0)
                mom_y = mom_y + jnp.sum(vy_hat * kept + step_y * (up_y - down_y), axis=0)
                mom_y = mom_y - vy_hat_edge * (lost_up + lost_down)
            return total, mom_x, mom_y

        zero = jnp.zeros((8, 128), F32)
        total, mom_x, mom_y = lax.fori_loop(0, PACK, body, (zero, zero, zero))
        lost_up = jnp.where(i == KX - 1, 1.0, 0.0) * upx[BX]
        lost_down = jnp.where(i == 0, 1.0, 0.0) * dnx[1]
        s_up, s_down = jnp.sum(lost_up, axis=0), jnp.sum(lost_down, axis=0)
        total = total - (s_up + s_down)
        mom_x = mom_x - vx_hat(jnp.int32(BX)) * s_up - vx_hat(jnp.int32(-1)) * s_down
        mom_y = mom_y - jnp.sum(vy_hat * (lost_up + lost_down), axis=0)
        return total, mom_x, mom_y

    def inflow(ext, hslot, stats, write, cslot):
        total, mean_x, mean_y = stats
        x_rates(ext, 0, mean_x)
        x_rates(ext, BX + 1, mean_x)

        def body(q, _):
            face = None
            for b in range(PACK):
                vx = PACK * q + b
                drift = drift_limit * jnp.tanh(mean_y - vy_hat_edge - gradh[vx])
                cells = hy[hslot, vx]
                up_edge = cells * (diffusion + jnp.maximum(drift, 0.0))
                down_edge = cells * (diffusion + jnp.maximum(-drift, 0.0))
                lower, upper = vy_neighbours(upy[vx], dny[vx], up_edge, down_edge)
                new = base[vx] + upx[vx] + dnx[vx + 2] + lower + upper
                write(vx, new)
                face = packed(face, new, b)
            turn(cslot, q, face)
            return 0

        lax.fori_loop(0, PACK, body, 0)

    vy_pack(2, lambda vx, t: mext[vx + 1, t])
    x_pack(1, lambda vx: mext[vx + 1], high_x)
    loads[2].wait()
    vy_pack(0, lambda vx, t: uext[vx + 1, t])
    x_pack(0, lambda vx: uext[vx + 1], jnp.logical_not(high_x))
    loads[3].wait()

    def fill_g(vx, _):
        gvy[0, vx] = gext[vx + 2, TILES - 1]
        gvy[1, vx] = gext[vx + 2, 0]
        return 0

    lax.fori_loop(0, BX, fill_g, 0)
    pl.semaphore_wait(barrier, len(roles))

    depth0 = depth_start(0)
    u_vy = vy_send(0)
    u_vx = vx_faces(uext)
    u_x = x_send(0, jnp.logical_not(high_x))
    m_vy = vy_send(2)
    g_vy = [start(gvy.at[0], gvy.at[2], vy_up), start(gvy.at[1], gvy.at[3], vy_down)]
    m_vx = vx_faces(mext)
    g_vx = [
        start(gext.at[pl.ds(BX, 2)], gext.at[pl.ds(0, 2)], vx_up),
        start(gext.at[pl.ds(2, 2)], gext.at[pl.ds(BX + 2, 2)], vx_down),
    ]
    m_x = x_send(1, high_x)
    plane0 = plane_start(0, depth0)

    vx_halo(uext, u_vx)
    vy_halo(0, u_vy)
    arrive([u_x])
    make_u = mirror_copies(0)

    def value_step(q, _):
        face = None
        for b in range(PACK):
            vx = PACK * q + b
            below, here, above = uext[vx], uext[vx + 1], uext[vx + 2]
            lower, upper = both_vy(here, hy[0, vx])
            grad_x = 0.5 * (above - below)
            grad_y = 0.5 * (upper - lower)
            laplace = above + below + upper + lower - 4.0 * here
            speed_x = jnp.abs(advect_rate * vx_hat(vx))
            moved = speed_x * (x_neighbour(here, 0, q, b, jnp.logical_not(high_x)) - here)
            moved = moved + speed_y * (y_neighbour(here, jnp.logical_not(high_y)) - here)
            new = here + moved - hamilton_rate * (grad_x * grad_x + grad_y * grad_y) + diffusion * laplace
            pre[vx] = new
            face = packed(face, new, b)
        turn(0, q, face)
        make_u(q).start()
        return 0

    lax.fori_loop(0, PACK, value_step, 0)

    arrive(g_vx)
    for s in range(2):
        gext[s] = jnp.where(i == 0, 0.0, gext[s])
        gext[BX + 2 + s] = jnp.where(i == KX - 1, 0.0, gext[BX + 2 + s])

    def grads_x(e, _):
        gradx[e] = 0.5 * (gext[e + 2] - gext[e])
        return 0

    lax.fori_loop(0, BX + 2, grads_x, 0)
    arrive(g_vy)

    def grads_y(vx, _):
        low = jnp.where(j == 0, 0.0, gvy[2, vx])
        high = jnp.where(j == KY - 1, 0.0, gvy[3, vx])
        slab = gext[vx + 2]
        edge = jnp.where(lo8, roll4(low), roll4(high))
        lower, upper = both_vy(slab, edge)
        grady[vx] = 0.5 * (upper - lower)
        gradh[vx] = jnp.where(lo8, 0.5 * (slab[0] - low), 0.5 * (high - slab[TILES - 1]))
        return 0

    lax.fori_loop(0, BX, grads_y, 0)

    vx_halo(mext, m_vx)
    vy_halo(2, m_vy)
    arrive([m_x])
    stats0 = plane_finish(0, plane0)
    outflow(mext, stats0)
    put_moments(20, stay(mext, 1), jnp.logical_not(wall))
    depth1 = depth_start(1)

    def write_field(vx, slab):
        field[vx] = slab

    inflow(mext, 1, stats0, write_field, 1)
    make_1 = mirror_copies(1)
    for q in range(EARLY[0]):
        make_1(q).start()

    def write_v(vx, slab):
        vext[vx + 1] = slab

    plane1 = plane_start(1, depth1)
    for q in range(EARLY[0], PACK):
        make_1(q).start()
    reflect(0, make_u, lambda vx: pre[vx], write_v)
    x_pack(2, lambda vx: vext[vx + 1], jnp.logical_not(high_x))
    v_x = x_send(2, jnp.logical_not(high_x))
    v_vx = vx_faces(vext)
    vy_pack(6, lambda vx, t: vext[vx + 1, t])
    v_vy = vy_send(6)

    arrive([v_x])
    make_z = mirror_copies(2)

    def transport_step(q, _):
        face = None
        for b in range(PACK):
            vx = PACK * q + b
            here = vext[vx + 1]
            speed_x = jnp.abs(advect_rate * vx_hat(vx))
            moved = speed_x * x_neighbour(here, 2, q, b, jnp.logical_not(high_x))
            moved = moved + speed_y * y_neighbour(here, jnp.logical_not(high_y))
            pre[vx] = moved
            face = packed(face, moved, b)
        turn(2, q, face)
        return 0

    lax.fori_loop(0, PACK, transport_step, 0)
    for q in range(PACK):
        make_z(q).start()

    def write_m(vx, slab):
        mext2[vx + 1] = slab

    reflect(1, make_1, lambda vx: field[vx], write_m)
    vy_pack(4, lambda vx, t: mext2[vx + 1, t])
    n_vy = vy_send(4)
    n_vx = vx_faces(mext2)
    x_pack(3, lambda vx: mext2[vx + 1], high_x)
    n_x = x_send(3, high_x)

    stats1 = plane_finish(1, plane1)
    outflow(mext2, stats1)
    arrive([n_x])
    put_moments(40, stay(mext2, 3), jnp.logical_not(wall))
    depth2 = depth_start(2)
    vx_halo(mext2, n_vx)
    vy_halo(4, n_vy)

    def write_out(vx, slab):
        mo_ref[vx] = slab

    inflow(mext2, 2, stats1, write_out, 3)
    make_2 = mirror_copies(3)
    for q in range(EARLY[1]):
        make_2(q).start()

    def write_z(vx, slab):
        wz[vx] = slab

    vx_halo(vext, v_vx)
    vy_halo(6, v_vy)
    plane2 = plane_start(2, depth2)
    for q in range(EARLY[1], PACK):
        make_2(q).start()
    reflect(2, make_z, lambda vx: pre[vx], write_z)
    total2, mean_x2, mean_y2 = plane_finish(2, plane2)

    half = 0.5 * time_step * velocity_cost

    def coefficients(total, mean_x, mean_y):
        density = time_step * density_cost * (total / (VX * VY))
        return density + half * (mean_x * mean_x + mean_y * mean_y), 2.0 * half * mean_x, 2.0 * half * mean_y

    c0, c1, c2 = coefficients(total2, mean_x2, mean_y2)
    e0, e1, e2 = coefficients(*stats1)
    for k, c in enumerate((c0, c1, c2)):
        tiles[k] = c
    back = jnp.logical_not(high_x)
    stats_copy = start(tiles.at[pl.ds(0, 3)], tiles.at[pl.ds(3, 3)], {"gx": jnp.where(back, (gx + 1) % gx_count, (gx + gx_count - 1) % gx_count)})
    edge_row = row % 4 == jnp.where(back, 0, 3)

    def x_tile(here):
        return jnp.where(back, pltpu.roll(here, 1, axis=0), pltpu.roll(here, 7, axis=0))

    def x_far(t):
        return jnp.where(back, pltpu.roll(tiles[3 + t], 5, axis=0), pltpu.roll(tiles[3 + t], 3, axis=0))

    down_y = jnp.logical_not(high_y)
    near = jnp.where(down_y, 1, 127)
    away = jnp.where(down_y, 127, 1)
    y_near = [pltpu.roll(c, near, axis=1) for c in (c0, c1, c2)]
    y_away = [pltpu.roll(c, away, axis=1) for c in (c0, c1, c2)]
    x0, x1, x2 = x_tile(c0), x_tile(c1), jnp.where(wall, 0.0, x_tile(c2))
    y0 = jnp.where(wall, 0.5 * (y_near[0] + y_away[0]), y_near[0])
    y1 = jnp.where(wall, 0.5 * (y_near[1] + y_away[1]), y_near[1])
    y2 = jnp.where(wall, 0.5 * (y_near[2] - y_away[2]), y_near[2])

    def cost(k0, k1, k2, vxh, vyh):
        return k0 - k1 * vxh - k2 * vyh + half * (vxh * vxh + vyh * vyh)

    def last_step(vx, _):
        vxh, vxh_low, vxh_high = vx_hat(vx), vx_hat(vx - 1), vx_hat(vx + 1)
        run_v = half * vy_hat * vy_hat - c2[None] * vy_hat + c0[None]
        run = (half * vxh * vxh - c1 * vxh)[None] + run_v
        has_low = (i * BX + vx) > 0
        has_high = (i * BX + vx) < VX - 1
        here = vext[vx + 1] + run
        below = vext[vx] + jnp.where(has_low, (half * vxh_low * vxh_low - c1 * vxh_low)[None] + run_v, 0.0)
        above = vext[vx + 2] + jnp.where(has_high, (half * vxh_high * vxh_high - c1 * vxh_high)[None] + run_v, 0.0)
        edge = hy[3, vx] + jnp.where(inside_edge, cost(c0, c1, c2, vxh, vy_hat_edge), 0.0)
        lower, upper = both_vy(here, edge)
        grad_x = 0.5 * (above - below)
        grad_y = 0.5 * (upper - lower)
        laplace = above + below + upper + lower - 4.0 * here
        speed_x = jnp.abs(advect_rate * vxh)
        inner = speed_x * cost(x0[None], x1[None], x2[None], vxh, vy_hat)
        moved = wz[vx] + jnp.where(edge_row[None], 0.0, inner)
        moved = moved + speed_y * cost(y0[None], y1[None], y2[None], vxh, vy_hat)
        moved = moved - (speed_x + speed_y) * here
        new = here + moved - hamilton_rate * (grad_x * grad_x + grad_y * grad_y) + diffusion * laplace
        vo_ref[vx] = new + cost(e0[None], e1[None], e2[None], vxh, vy_hat)
        return 0

    lax.fori_loop(0, BX, last_step, 0)

    def edge_part():
        arrive([stats_copy])
        f0, f1, f2 = x_far(0), x_far(1), jnp.where(wall, 0.0, x_far(2))

        def edge_step(vx, _):
            vxh = vx_hat(vx)
            outer = jnp.abs(advect_rate * vxh) * cost(f0[None], f1[None], f2[None], vxh, vy_hat)
            vo_ref[vx] = vo_ref[vx] + jnp.where(edge_row[None], outer, 0.0)
            return 0

        lax.fori_loop(0, BX, edge_step, 0)

    def write_end(vx, slab):
        mo_ref[vx] = slab

    reflect(3, make_2, lambda vx: mo_ref[vx], write_end)
    edge_part()

    for c in sent:
        c.wait_send()
    for make in (make_u, make_1, make_z, make_2):
        for q in range(PACK):
            make(q).wait_send()


def per_device(density_start, value_guess, value_end, walls):
    field_shape = (BX, TILES, 8, 128)

    def tiled(a):
        return a.reshape(field_shape)

    vmem = pl.BlockSpec(memory_space=pltpu.VMEM)

    def slabs(n):
        return pltpu.VMEM((n, TILES, 8, 128), F32)

    def stacks(n, m):
        return pltpu.VMEM((n, m, TILES, 8, 128), F32)

    out = jax.ShapeDtypeStruct(field_shape, F32)
    density_end, value_start = pl.pallas_call(
        kernel,
        out_shape=(out, out),
        in_specs=[pl.BlockSpec(memory_space=pltpu.HBM)] * 4,
        out_specs=(vmem, vmem),
        scratch_shapes=[
            slabs(18), slabs(18), slabs(20), slabs(18), slabs(16),
            pltpu.VMEM((16, 8, 128), F32),
            slabs(18), slabs(18), slabs(16), slabs(16), slabs(16),
            slabs(16), slabs(18), slabs(18), slabs(16), slabs(16),
            pltpu.VMEM((4, 16, 8, 128), F32),
            stacks(4, 4),
            pltpu.VMEM((4, 8, 8, 128), F32), pltpu.VMEM((4, 8, 8, 128), F32),
            pltpu.VMEM((8, 8, 8, 128), F32),
            stacks(4, 4),
            pltpu.VMEM((4, 16, 8, 128), F32),
            stacks(4, 4), stacks(4, 4),
            pltpu.VMEM((60, 2, 8, 128), F32),
            pltpu.VMEM((6, 8, 128), F32),
            pltpu.VMEM((2, 8, 128), jnp.int32),
            pltpu.VMEM((4, 128), jnp.int32),
            pltpu.SemaphoreType.DMA((112,)),
            pltpu.SemaphoreType.DMA((112,)),
            pltpu.SemaphoreType.DMA((4,)),
        ],
        compiler_params=pltpu.CompilerParams(
            collective_id=0, has_side_effects=True, vmem_limit_bytes=60 * 1024 * 1024
        ),
    )(tiled(density_start), tiled(value_guess), tiled(value_end), walls)
    return density_end.reshape(density_start.shape), value_start.reshape(density_start.shape)


def solution(mesh):
    return jax.shard_map(
        per_device,
        mesh=mesh,
        in_specs=(
            P("vert", None, None, "gx", None),
            P("vert", None, None, "gx", None),
            P("vert", None, None, "gx", None),
            P("gx", None),
        ),
        out_specs=(P("vert", None, None, "gx", None), P("vert", None, None, "gx", None)),
        check_vma=False,
    )
```

```python
import functools

import jax
import jax.numpy as jnp
from jax import lax
from jax.experimental import pallas as pl
from jax.experimental.pallas import tpu as pltpu
from jax.sharding import PartitionSpec as P

MESH = pl.DeviceIdType.MESH
F32 = jnp.float32

VX = 128
VY = 128
KX = 8
KY = 8
BX = 16
BY = 16
TILES = 8
EARLY = (3, 1)
PACK = 4

advect_rate = 0.3
diffusion = 0.05
drift_limit = 0.1
hamilton_rate = 0.05
time_step = 0.2
density_cost = 2.0
velocity_cost = 1.0


def roll4(a):
    return pltpu.roll(a, 4, axis=a.ndim - 2)


def kernel(
    m_hbm, g_hbm, u_hbm, walls_hbm, mo_ref, vo_ref,
    mext, mext2, gext, gradx, grady, gradh, upx, dnx, upy, dny, base, field, uext, vext, pre, wz,
    hy, xh, ylo, yhi, ysend, xsend, gvy, csend, crecv, red, tiles, idx, walls_ref,
    send_sem, recv_sem, load_sem,
):
    vert = lax.axis_index("vert")
    gx = lax.axis_index("gx")
    gx_count = lax.axis_size("gx")
    i = vert // KY
    j = vert % KY
    zh = vert % 4
    px = (vert // 4) % 4
    py = vert // 16

    def at(y, x, z):
        return {"vert": ((y % 4) * 4 + x % 4) * 4 + z % 4}

    plane = [at(py + d // 4, px + d % 4, zh) for d in range(1, 16)]
    depth = [at(py, px, zh + d) for d in range(1, 4)]
    mirror = {"vert": i * KY + (KY - 1 - j)}
    vx_up = {"vert": ((i + 1) % KX) * KY + j}
    vx_down = {"vert": ((i + KX - 1) % KX) * KY + j}
    vy_up = {"vert": i * KY + (j + 1) % KY}
    vy_down = {"vert": i * KY + (j + KY - 1) % KY}
    x_up = {"gx": (gx + 1) % gx_count}
    x_down = {"gx": (gx + gx_count - 1) % gx_count}

    loads = [
        pltpu.make_async_copy(m_hbm, mext.at[pl.ds(1, BX)], load_sem.at[0]),
        pltpu.make_async_copy(walls_hbm, walls_ref, load_sem.at[1]),
        pltpu.make_async_copy(u_hbm, uext.at[pl.ds(1, BX)], load_sem.at[2]),
        pltpu.make_async_copy(g_hbm, gext.at[pl.ds(2, BX)], load_sem.at[3]),
    ]
    for load in loads:
        load.start()

    barrier = pltpu.get_barrier_semaphore()
    roles = depth + [mirror, vy_up, vy_down] + plane + [x_up, x_down]
    for peer in roles:
        pl.semaphore_signal(barrier, inc=1, device_id=peer, device_id_type=MESH)

    row = lax.broadcasted_iota(jnp.int32, (8, 128), 0)
    lane = lax.broadcasted_iota(jnp.int32, (8, 128), 1)
    lo8 = row < 4
    high_x = i >= KX // 2
    high_y = j >= KY // 2

    def vx_hat(e):
        return ((i * BX + e).astype(F32) - (VX - 1) / 2.0) / (VX / 2.0)

    shape = (TILES, 8, 128)
    vy_row = 2 * lax.broadcasted_iota(jnp.int32, shape, 0) + lax.broadcasted_iota(jnp.int32, shape, 1) // 4
    vy_hat = ((j * BY + vy_row).astype(F32) - (VY - 1) / 2.0) / (VY / 2.0)
    vy_edge = jnp.where(lo8, j * BY - 1, j * BY + BY)
    vy_hat_edge = (vy_edge.astype(F32) - (VY - 1) / 2.0) / (VY / 2.0)
    inside_edge = (vy_edge >= 0) & (vy_edge < VY)
    speed_y = jnp.abs(advect_rate * vy_hat)

    def local_moments(read):
        def body(vx, carry):
            total, mom_x, mom_y = carry
            slab = read(vx)
            s = jnp.sum(slab, axis=0)
            return (total + s, mom_x + vx_hat(vx) * s, mom_y + jnp.sum(vy_hat * slab, axis=0))

        zero = jnp.zeros((8, 128), F32)
        return lax.fori_loop(0, BX, body, (zero, zero, zero))

    def put_moments(slot, sums, mom_y_cells=None):
        total, mom_x, mom_y = (a + roll4(a) for a in sums)
        if mom_y_cells is not None:
            mom_y = jnp.where(mom_y_cells, mom_y, 0.0)
        red[slot, 0] = jnp.where(lo8, total, mom_x)
        red[slot, 1] = mom_y

    loads[0].wait()
    put_moments(0, local_moments(lambda vx: mext[vx + 1]))

    loads[1].wait()
    w4 = walls_ref[...]
    wall = jnp.concatenate([w4, w4], axis=0) == 1
    ones = wall.astype(F32)
    sub128 = lax.broadcasted_iota(jnp.int32, (128, 128), 0)
    lane128 = lax.broadcasted_iota(jnp.int32, (128, 128), 1)
    upto = (sub128 <= lane128).astype(F32)
    count = jnp.dot(ones, upto, preferred_element_type=F32)
    count_t = lax.dot_general(
        (lane128 <= sub128).astype(F32), ones, (((1,), (1,)), ((), ())), preferred_element_type=F32
    )
    rank = jnp.clip(count.astype(jnp.int32) - 1, 0, 31)
    nth = (lane128 % 32).astype(F32)
    pick = jnp.zeros((8, 128), F32)
    for x in range(4):
        place = jnp.sum((count_t[:, x : x + 1] <= nth).astype(F32), axis=0, keepdims=True)
        pick = jnp.where(row % 4 == x, place, pick)
    idx[0] = jnp.minimum(pick.astype(jnp.int32), 127)
    idx[1] = rank

    def along_y(slab, index):
        return jnp.take_along_axis(slab, jnp.broadcast_to(index[None], shape), axis=2)


    counter = [0]

    def copy(src, dst, peer):
        n = counter[0]
        counter[0] += 1
        return pltpu.make_async_remote_copy(
            src_ref=src, dst_ref=dst, send_sem=send_sem.at[n], recv_sem=recv_sem.at[n],
            device_id=peer, device_id_type=MESH,
        )

    sent = []

    def start(src, dst, peer):
        c = copy(src, dst, peer)
        c.start()
        sent.append(c)
        return c

    def arrive(copies):
        for c in copies:
            c.wait_recv()

    def depth_start(r):
        base = 20 * r
        return [start(red.at[base], red.at[base + 1 + d], peer) for d, peer in enumerate(depth)]

    def plane_start(r, copies):
        base = 20 * r
        arrive(copies)
        acc = red[base]
        for d in range(3):
            acc = acc + red[base + 1 + d]
        red[base + 4] = acc
        return [start(red.at[base + 4], red.at[base + 5 + d], peer) for d, peer in enumerate(plane)]

    def plane_finish(r, copies):
        base = 20 * r
        arrive(copies)
        acc = red[base + 4]
        for d in range(15):
            acc = acc + red[base + 5 + d]
        swapped = roll4(acc[0])
        total = jnp.where(lo8, acc[0], swapped)
        mom_x = jnp.where(lo8, swapped, acc[0])
        return total, mom_x / total, acc[1] / total

    def vy_pack(slot, read):
        def body(p, _):
            a0, a1 = read(2 * p, TILES - 1), read(2 * p + 1, TILES - 1)
            ysend[slot, p] = jnp.where(lo8, roll4(a0), a1)
            b0, b1 = read(2 * p, 0), read(2 * p + 1, 0)
            ysend[slot + 1, p] = jnp.where(lo8, b0, roll4(b1))
            return 0

        lax.fori_loop(0, BX // 2, body, 0)

    def vy_send(slot):
        return [
            start(ysend.at[slot], ylo.at[slot // 2], vy_up),
            start(ysend.at[slot + 1], yhi.at[slot // 2], vy_down),
        ]

    def vy_halo(slot, copies):
        arrive(copies)

        def body(p, _):
            low, high = ylo[slot // 2, p], yhi[slot // 2, p]
            hy[slot // 2, 2 * p] = jnp.where(inside_edge, jnp.where(lo8, low, roll4(high)), 0.0)
            hy[slot // 2, 2 * p + 1] = jnp.where(inside_edge, jnp.where(lo8, roll4(low), high), 0.0)
            return 0

        lax.fori_loop(0, BX // 2, body, 0)

    def vx_faces(ext):
        return [
            start(ext.at[BX], ext.at[0], vx_up),
            start(ext.at[1], ext.at[BX + 1], vx_down),
        ]

    def vx_halo(ext, copies):
        arrive(copies)
        ext[0] = jnp.where(i == 0, 0.0, ext[0])
        ext[BX + 1] = jnp.where(i == KX - 1, 0.0, ext[BX + 1])

    def x_pack(slot, read, below):
        def body(q, _):
            face = None
            for b in range(PACK):
                slab = read(PACK * q + b)
                moved = jnp.where(below, pltpu.roll(slab, (b - 3) % 8, axis=1), pltpu.roll(slab, (b + 3) % 8, axis=1))
                target = jnp.where(below, b, b + 3) % 4
                face = moved if face is None else jnp.where((row % 4 == target)[None], moved, face)
            xsend[slot, q] = face
            return 0

        lax.fori_loop(0, BX // PACK, body, 0)

    def x_neighbour(slab, slot, q, b, below):
        shifted = jnp.where(below, pltpu.roll(slab, 1, axis=1), pltpu.roll(slab, 7, axis=1))
        edge = row % 4 == jnp.where(below, 0, 3)
        return jnp.where(edge[None], pltpu.roll(xh[slot, q], (8 - b) % 8, axis=1), shifted)

    def y_neighbour(slab, below):
        return pltpu.roll(slab, jnp.where(below, 1, 127), axis=2)

    def vy_neighbours(low, high, edge_low, edge_high):
        r_low, r_high = roll4(low), roll4(high)
        lower = jnp.where(lo8[None], jnp.concatenate([edge_low[None], r_low[:-1]], axis=0), r_low)
        upper = jnp.where(lo8[None], r_high, jnp.concatenate([r_high[1:], edge_high[None]], axis=0))
        return lower, upper

    def both_vy(slab, edge):
        r = roll4(slab)
        lower = jnp.where(lo8[None], jnp.concatenate([edge[None], r[:-1]], axis=0), r)
        upper = jnp.where(lo8[None], r, jnp.concatenate([r[1:], edge[None]], axis=0))
        return lower, upper

    def x_send(slot, below):
        peer = {"gx": jnp.where(below, (gx + 1) % gx_count, (gx + gx_count - 1) % gx_count)}
        return start(xsend.at[slot], xh.at[slot], peer)

    def mirror_copies(slot):
        n = counter[0]
        counter[0] += PACK

        def make(q):
            return pltpu.make_async_remote_copy(
                src_ref=csend.at[slot, q], dst_ref=crecv.at[slot, q],
                send_sem=send_sem.at[n + q], recv_sem=recv_sem.at[n + q],
                device_id=mirror, device_id_type=MESH,
            )

        return make

    def packed(face, slab, b):
        taken = along_y(slab, idx[0])
        return taken if face is None else jnp.where((lane // 32 == b)[None], taken, face)

    def turn(slot, q, face):
        turned = roll4(face)
        for t in range(TILES):
            csend[slot, q, t] = turned[TILES - 1 - t]

    def reflect(slot, make, read, write):
        def body(q, carry):
            make(q).wait_recv()
            face = crecv[slot, q]
            for b in range(PACK):
                vx = PACK * q + b
                slab = read(vx)
                other = along_y(face, idx[1] + 32 * b)
                write(vx, jnp.where(wall[None], 0.5 * (slab + other), slab))
            return carry

        lax.fori_loop(0, PACK, body, 0)

    def x_rates(ext, e, mean_x):
        cells = ext[e]
        drift = drift_limit * jnp.tanh((mean_x - vx_hat(e - 1))[None] - gradx[e])
        upx[e] = cells * (diffusion + jnp.maximum(drift, 0.0))
        dnx[e] = cells * (diffusion + jnp.maximum(-drift, 0.0))

    def outflow(ext, stats):
        total, mean_x, mean_y = stats

        def body(vx, _):
            x_rates(ext, vx + 1, mean_x)
            cells = ext[vx + 1]
            drift = drift_limit * jnp.tanh(mean_y[None] - vy_hat - grady[vx])
            upy[vx] = cells * (diffusion + jnp.maximum(drift, 0.0))
            dny[vx] = cells * (diffusion + jnp.maximum(-drift, 0.0))
            return 0

        lax.fori_loop(0, BX, body, 0)

    def stay(ext, xslot):
        step_x, step_y = 2.0 / VX, 2.0 / VY
        top_y = jnp.where(jnp.logical_and(j == KY - 1, row >= 4), 1.0, 0.0)
        bottom_y = jnp.where(jnp.logical_and(j == 0, row < 4), 1.0, 0.0)

        def body(q, carry):
            total, mom_x, mom_y = carry
            for b in range(PACK):
                vx = PACK * q + b
                cells = ext[vx + 1]
                up_x, down_x, up_y, down_y = upx[vx + 1], dnx[vx + 1], upy[vx], dny[vx]
                speed_x = jnp.abs(advect_rate * vx_hat(vx))
                moved = speed_x * (cells - x_neighbour(cells, xslot, q, b, high_x))
                moved = moved + speed_y * (cells - y_neighbour(cells, high_y))
                kept = cells - moved
                base[vx] = kept - (up_x + down_x + up_y + down_y)
                s = jnp.sum(kept, axis=0)
                lost_up, lost_down = top_y * up_y[TILES - 1], bottom_y * down_y[0]
                total = total + s - (lost_up + lost_down)
                mom_x = mom_x + vx_hat(vx) * (s - (lost_up + lost_down)) + step_x * jnp.sum(up_x - down_x, axis=0)
                mom_y = mom_y + jnp.sum(vy_hat * kept + step_y * (up_y - down_y), axis=0)
                mom_y = mom_y - vy_hat_edge * (lost_up + lost_down)
            return total, mom_x, mom_y

        zero = jnp.zeros((8, 128), F32)
        total, mom_x, mom_y = lax.fori_loop(0, PACK, body, (zero, zero, zero))
        lost_up = jnp.where(i == KX - 1, 1.0, 0.0) * upx[BX]
        lost_down = jnp.where(i == 0, 1.0, 0.0) * dnx[1]
        s_up, s_down = jnp.sum(lost_up, axis=0), jnp.sum(lost_down, axis=0)
        total = total - (s_up + s_down)
        mom_x = mom_x - vx_hat(jnp.int32(BX)) * s_up - vx_hat(jnp.int32(-1)) * s_down
        mom_y = mom_y - jnp.sum(vy_hat * (lost_up + lost_down), axis=0)
        return total, mom_x, mom_y

    def inflow(ext, hslot, stats, write, cslot):
        total, mean_x, mean_y = stats
        x_rates(ext, 0, mean_x)
        x_rates(ext, BX + 1, mean_x)

        def body(q, _):
            face = None
            for b in range(PACK):
                vx = PACK * q + b
                drift = drift_limit * jnp.tanh(mean_y - vy_hat_edge - gradh[vx])
                cells = hy[hslot, vx]
                up_edge = cells * (diffusion + jnp.maximum(drift, 0.0))
                down_edge = cells * (diffusion + jnp.maximum(-drift, 0.0))
                lower, upper = vy_neighbours(upy[vx], dny[vx], up_edge, down_edge)
                new = base[vx] + upx[vx] + dnx[vx + 2] + lower + upper
                write(vx, new)
                face = packed(face, new, b)
            turn(cslot, q, face)
            return 0

        lax.fori_loop(0, PACK, body, 0)

    vy_pack(2, lambda vx, t: mext[vx + 1, t])
    x_pack(1, lambda vx: mext[vx + 1], high_x)
    loads[2].wait()
    vy_pack(0, lambda vx, t: uext[vx + 1, t])
    x_pack(0, lambda vx: uext[vx + 1], jnp.logical_not(high_x))
    loads[3].wait()

    def fill_g(vx, _):
        gvy[0, vx] = gext[vx + 2, TILES - 1]
        gvy[1, vx] = gext[vx + 2, 0]
        return 0

    lax.fori_loop(0, BX, fill_g, 0)
    pl.semaphore_wait(barrier, len(roles))

    depth0 = depth_start(0)
    u_vy = vy_send(0)
    u_vx = vx_faces(uext)
    u_x = x_send(0, jnp.logical_not(high_x))
    m_vy = vy_send(2)
    g_vy = [start(gvy.at[0], gvy.at[2], vy_up), start(gvy.at[1], gvy.at[3], vy_down)]
    m_vx = vx_faces(mext)
    g_vx = [
        start(gext.at[pl.ds(BX, 2)], gext.at[pl.ds(0, 2)], vx_up),
        start(gext.at[pl.ds(2, 2)], gext.at[pl.ds(BX + 2, 2)], vx_down),
    ]
    m_x = x_send(1, high_x)
    plane0 = plane_start(0, depth0)

    vx_halo(uext, u_vx)
    vy_halo(0, u_vy)
    arrive([u_x])
    make_u = mirror_copies(0)

    def value_step(q, _):
        face = None
        for b in range(PACK):
            vx = PACK * q + b
            below, here, above = uext[vx], uext[vx + 1], uext[vx + 2]
            lower, upper = both_vy(here, hy[0, vx])
            grad_x = 0.5 * (above - below)
            grad_y = 0.5 * (upper - lower)
            laplace = above + below + upper + lower - 4.0 * here
            speed_x = jnp.abs(advect_rate * vx_hat(vx))
            moved = speed_x * (x_neighbour(here, 0, q, b, jnp.logical_not(high_x)) - here)
            moved = moved + speed_y * (y_neighbour(here, jnp.logical_not(high_y)) - here)
            new = here + moved - hamilton_rate * (grad_x * grad_x + grad_y * grad_y) + diffusion * laplace
            pre[vx] = new
            face = packed(face, new, b)
        turn(0, q, face)
        make_u(q).start()
        return 0

    lax.fori_loop(0, PACK, value_step, 0)

    arrive(g_vx)
    for s in range(2):
        gext[s] = jnp.where(i == 0, 0.0, gext[s])
        gext[BX + 2 + s] = jnp.where(i == KX - 1, 0.0, gext[BX + 2 + s])

    def grads_x(e, _):
        gradx[e] = 0.5 * (gext[e + 2] - gext[e])
        return 0

    lax.fori_loop(0, BX + 2, grads_x, 0)
    arrive(g_vy)

    def grads_y(vx, _):
        low = jnp.where(j == 0, 0.0, gvy[2, vx])
        high = jnp.where(j == KY - 1, 0.0, gvy[3, vx])
        slab = gext[vx + 2]
        edge = jnp.where(lo8, roll4(low), roll4(high))
        lower, upper = both_vy(slab, edge)
        grady[vx] = 0.5 * (upper - lower)
        gradh[vx] = jnp.where(lo8, 0.5 * (slab[0] - low), 0.5 * (high - slab[TILES - 1]))
        return 0

    lax.fori_loop(0, BX, grads_y, 0)

    vx_halo(mext, m_vx)
    vy_halo(2, m_vy)
    arrive([m_x])
    stats0 = plane_finish(0, plane0)
    outflow(mext, stats0)
    put_moments(20, stay(mext, 1), jnp.logical_not(wall))
    depth1 = depth_start(1)

    def write_field(vx, slab):
        field[vx] = slab

    inflow(mext, 1, stats0, write_field, 1)
    make_1 = mirror_copies(1)
    for q in range(EARLY[0]):
        make_1(q).start()

    def write_v(vx, slab):
        vext[vx + 1] = slab

    plane1 = plane_start(1, depth1)
    for q in range(EARLY[0], PACK):
        make_1(q).start()
    reflect(0, make_u, lambda vx: pre[vx], write_v)
    x_pack(2, lambda vx: vext[vx + 1], jnp.logical_not(high_x))
    v_x = x_send(2, jnp.logical_not(high_x))
    v_vx = vx_faces(vext)
    vy_pack(6, lambda vx, t: vext[vx + 1, t])
    v_vy = vy_send(6)

    arrive([v_x])
    make_z = mirror_copies(2)

    def transport_step(q, _):
        face = None
        for b in range(PACK):
            vx = PACK * q + b
            here = vext[vx + 1]
            speed_x = jnp.abs(advect_rate * vx_hat(vx))
            moved = speed_x * x_neighbour(here, 2, q, b, jnp.logical_not(high_x))
            moved = moved + speed_y * y_neighbour(here, jnp.logical_not(high_y))
            pre[vx] = moved
            face = packed(face, moved, b)
        turn(2, q, face)
        return 0

    lax.fori_loop(0, PACK, transport_step, 0)
    for q in range(PACK):
        make_z(q).start()

    def write_m(vx, slab):
        mext2[vx + 1] = slab

    reflect(1, make_1, lambda vx: field[vx], write_m)
    vy_pack(4, lambda vx, t: mext2[vx + 1, t])
    n_vy = vy_send(4)
    n_vx = vx_faces(mext2)
    x_pack(3, lambda vx: mext2[vx + 1], high_x)
    n_x = x_send(3, high_x)

    stats1 = plane_finish(1, plane1)
    outflow(mext2, stats1)
    arrive([n_x])
    put_moments(40, stay(mext2, 3), jnp.logical_not(wall))
    depth2 = depth_start(2)
    vx_halo(mext2, n_vx)
    vy_halo(4, n_vy)

    def write_out(vx, slab):
        mo_ref[vx] = slab

    inflow(mext2, 2, stats1, write_out, 3)
    make_2 = mirror_copies(3)
    for q in range(EARLY[1]):
        make_2(q).start()

    def write_z(vx, slab):
        wz[vx] = slab

    vx_halo(vext, v_vx)
    vy_halo(6, v_vy)
    plane2 = plane_start(2, depth2)
    for q in range(EARLY[1], PACK):
        make_2(q).start()
    reflect(2, make_z, lambda vx: pre[vx], write_z)
    total2, mean_x2, mean_y2 = plane_finish(2, plane2)

    half = 0.5 * time_step * velocity_cost

    def coefficients(total, mean_x, mean_y):
        density = time_step * density_cost * (total / (VX * VY))
        return density + half * (mean_x * mean_x + mean_y * mean_y), 2.0 * half * mean_x, 2.0 * half * mean_y

    c0, c1, c2 = coefficients(total2, mean_x2, mean_y2)
    e0, e1, e2 = coefficients(*stats1)
    for k, c in enumerate((c0, c1, c2)):
        tiles[k] = c
    back = jnp.logical_not(high_x)
    stats_copy = start(tiles.at[pl.ds(0, 3)], tiles.at[pl.ds(3, 3)], {"gx": jnp.where(back, (gx + 1) % gx_count, (gx + gx_count - 1) % gx_count)})
    edge_row = row % 4 == jnp.where(back, 0, 3)

    def x_tile(here):
        return jnp.where(back, pltpu.roll(here, 1, axis=0), pltpu.roll(here, 7, axis=0))

    def x_far(t):
        return jnp.where(back, pltpu.roll(tiles[3 + t], 5, axis=0), pltpu.roll(tiles[3 + t], 3, axis=0))

    down_y = jnp.logical_not(high_y)
    near = jnp.where(down_y, 1, 127)
    away = jnp.where(down_y, 127, 1)
    y_near = [pltpu.roll(c, near, axis=1) for c in (c0, c1, c2)]
    y_away = [pltpu.roll(c, away, axis=1) for c in (c0, c1, c2)]
    x0, x1, x2 = x_tile(c0), x_tile(c1), jnp.where(wall, 0.0, x_tile(c2))
    y0 = jnp.where(wall, 0.5 * (y_near[0] + y_away[0]), y_near[0])
    y1 = jnp.where(wall, 0.5 * (y_near[1] + y_away[1]), y_near[1])
    y2 = jnp.where(wall, 0.5 * (y_near[2] - y_away[2]), y_near[2])

    def cost(k0, k1, k2, vxh, vyh):
        return k0 - k1 * vxh - k2 * vyh + half * (vxh * vxh + vyh * vyh)

    def last_step(vx, _):
        vxh, vxh_low, vxh_high = vx_hat(vx), vx_hat(vx - 1), vx_hat(vx + 1)
        run_v = half * vy_hat * vy_hat - c2[None] * vy_hat + c0[None]
        run = (half * vxh * vxh - c1 * vxh)[None] + run_v
        has_low = (i * BX + vx) > 0
        has_high = (i * BX + vx) < VX - 1
        here = vext[vx + 1] + run
        below = vext[vx] + jnp.where(has_low, (half * vxh_low * vxh_low - c1 * vxh_low)[None] + run_v, 0.0)
        above = vext[vx + 2] + jnp.where(has_high, (half * vxh_high * vxh_high - c1 * vxh_high)[None] + run_v, 0.0)
        edge = hy[3, vx] + jnp.where(inside_edge, cost(c0, c1, c2, vxh, vy_hat_edge), 0.0)
        lower, upper = both_vy(here, edge)
        grad_x = 0.5 * (above - below)
        grad_y = 0.5 * (upper - lower)
        laplace = above + below + upper + lower - 4.0 * here
        speed_x = jnp.abs(advect_rate * vxh)
        inner = speed_x * cost(x0[None], x1[None], x2[None], vxh, vy_hat)
        moved = wz[vx] + jnp.where(edge_row[None], 0.0, inner)
        moved = moved + speed_y * cost(y0[None], y1[None], y2[None], vxh, vy_hat)
        moved = moved - (speed_x + speed_y) * here
        new = here + moved - hamilton_rate * (grad_x * grad_x + grad_y * grad_y) + diffusion * laplace
        vo_ref[vx] = new + cost(e0[None], e1[None], e2[None], vxh, vy_hat)
        return 0

    lax.fori_loop(0, BX, last_step, 0)

    def edge_part():
        arrive([stats_copy])
        f0, f1, f2 = x_far(0), x_far(1), jnp.where(wall, 0.0, x_far(2))

        def edge_step(vx, _):
            vxh = vx_hat(vx)
            outer = jnp.abs(advect_rate * vxh) * cost(f0[None], f1[None], f2[None], vxh, vy_hat)
            vo_ref[vx] = vo_ref[vx] + jnp.where(edge_row[None], outer, 0.0)
            return 0

        lax.fori_loop(0, BX, edge_step, 0)

    def write_end(vx, slab):
        mo_ref[vx] = slab

    reflect(3, make_2, lambda vx: mo_ref[vx], write_end)
    edge_part()

    for c in sent:
        c.wait_send()
    for make in (make_u, make_1, make_z, make_2):
        for q in range(PACK):
            make(q).wait_send()


def per_device(density_start, value_guess, value_end, walls):
    field_shape = (BX, TILES, 8, 128)

    def tiled(a):
        return a.reshape(field_shape)

    vmem = pl.BlockSpec(memory_space=pltpu.VMEM)

    def slabs(n):
        return pltpu.VMEM((n, TILES, 8, 128), F32)

    def stacks(n, m):
        return pltpu.VMEM((n, m, TILES, 8, 128), F32)

    out = jax.ShapeDtypeStruct(field_shape, F32)
    density_end, value_start = pl.pallas_call(
        kernel,
        out_shape=(out, out),
        in_specs=[pl.BlockSpec(memory_space=pltpu.HBM)] * 4,
        out_specs=(vmem, vmem),
        scratch_shapes=[
            slabs(18), slabs(18), slabs(20), slabs(18), slabs(16),
            pltpu.VMEM((16, 8, 128), F32),
            slabs(18), slabs(18), slabs(16), slabs(16), slabs(16),
            slabs(16), slabs(18), slabs(18), slabs(16), slabs(16),
            pltpu.VMEM((4, 16, 8, 128), F32),
            stacks(4, 4),
            pltpu.VMEM((4, 8, 8, 128), F32), pltpu.VMEM((4, 8, 8, 128), F32),
            pltpu.VMEM((8, 8, 8, 128), F32),
            stacks(4, 4),
            pltpu.VMEM((4, 16, 8, 128), F32),
            stacks(4, 4), stacks(4, 4),
            pltpu.VMEM((60, 2, 8, 128), F32),
            pltpu.VMEM((6, 8, 128), F32),
            pltpu.VMEM((2, 8, 128), jnp.int32),
            pltpu.VMEM((4, 128), jnp.int32),
            pltpu.SemaphoreType.DMA((112,)),
            pltpu.SemaphoreType.DMA((112,)),
            pltpu.SemaphoreType.DMA((4,)),
        ],
        compiler_params=pltpu.CompilerParams(
            collective_id=0, has_side_effects=True, vmem_limit_bytes=53 * 1024 * 1024
        ),
    )(tiled(density_start), tiled(value_guess), tiled(value_end), walls)
    return density_end.reshape(density_start.shape), value_start.reshape(density_start.shape)


def solution(mesh):
    return jax.shard_map(
        per_device,
        mesh=mesh,
        in_specs=(
            P("vert", None, None, "gx", None),
            P("vert", None, None, "gx", None),
            P("vert", None, None, "gx", None),
            P("gx", None),
        ),
        out_specs=(P("vert", None, None, "gx", None), P("vert", None, None, "gx", None)),
        check_vma=False,
    )
```
